128 devices in a mesh: ctx: 32 (over y, x, core), head: 4 (over z).
Axes of the slice: x: 4, y: 4, z: 4, core: 2. Of those that a mesh axis runs over, the one named last changes fastest.
Arguments:
- query_rows: bfloat16 [16384, 2048], P(('ctx', 'head')), may hold values from -6 to 6
- key_rows: bfloat16 [16384, 2048], P(('ctx', 'head')), may hold values from -6 to 6
- value_rows: bfloat16 [16384, 4096], P(('ctx', 'head')), may hold values from -6 to 6
- log_decay: bfloat16 [16384, 32], P(('ctx', 'head')), may hold values from -0.75 to 0, as said below
- beta_logit: bfloat16 [16384, 32], P(('ctx', 'head')), may hold values from -8 to 2
- out_grad: bfloat16 [16384, 4096], P(('ctx', 'head')), may hold values from -48 to 48
Outputs:
- query_grad: bfloat16 [16384, 2048], P(('ctx', 'head'))
- key_grad: bfloat16 [16384, 2048], P(('ctx', 'head'))
- value_grad: bfloat16 [16384, 4096], P(('ctx', 'head'))
- decay_grad: bfloat16 [16384, 32], P(('ctx', 'head'))
- beta_grad: bfloat16 [16384, 32], P(('ctx', 'head'))
The draws below stay inside these ranges and needn't reach their ends.
Inputs may be any that keep to these rules, and one draw needn't show every extreme that they name: `log_decay`: log decays are negative.
All inputs are finite; a program needn't handle non-finite values.
Results may differ from the reference program's by a relative error of at most 0.017.
Values may be sent and summed in bfloat16 or wider, within the bound.
No kernel may reach another device: no remote copies, remote signals or barrier semaphores. Data moves between devices by JAX's collectives and lax.ppermute only.
A program may use at most 256 MiB of HBM per device.

```python
import jax
import jax.numpy as jnp
from jax import lax

DK = 128
DV = 128
KH = 16
VH = 32
BLOCK = 64
TOKENS = 16384


def head_pace(key):
    return jax.random.uniform(jax.random.fold_in(key, 11), (VH,), jnp.float32)


def draw_log_decay(key, part):
    pace = head_pace(key)
    key = jax.random.fold_in(key, 1)
    first, second, third = jax.random.split(key, 3)
    lowest = jnp.log(0.3 / TOKENS)
    highest_rate = jnp.log(1.0 / 30.0)
    rate = jnp.exp(lowest + pace * (highest_rate - lowest))
    rough = jnp.exp(jax.random.uniform(first, (TOKENS, VH), jnp.float32, -0.7, 0.7))
    decay = -rate[None, :] * rough
    spots = jax.random.randint(second, (3,), 0, TOKENS)
    places = jnp.arange(TOKENS)
    struck = jnp.any(places[:, None] == spots[None, :], axis=1)
    loss = jax.random.uniform(third, (TOKENS, VH), jnp.float32, 0.5, 0.8)
    decay = jnp.where(struck[:, None], jnp.log(loss), decay)
    return decay.astype(jnp.bfloat16)


def draw_beta_logit(key, part):
    pace = head_pace(key)
    key = jax.random.fold_in(key, 2)
    lowest = jnp.log(0.5 * DK / TOKENS)
    highest_write = jnp.log(0.5)
    base = jnp.exp(lowest + pace * (highest_write - lowest))
    rough = jnp.exp(jax.random.uniform(key, (TOKENS, VH), jnp.float32, -0.5, 0.5))
    strength = base[None, :] * rough
    return (jnp.log(strength) - jnp.log1p(-strength)).astype(jnp.bfloat16)


def shard_levels(own_key, dims, cuts, low, largest):
    factor_of, own = 1.0, jax.random.fold_in(own_key, 6)
    for dim, shards_of in cuts:
        heights = jnp.exp(jax.random.uniform(jax.random.fold_in(own, dim), (shards_of,), jnp.float32, low / len(cuts), largest / len(cuts)))
        factor_of = factor_of * jnp.repeat(heights, dims[dim] // shards_of).reshape([-1 if axis == dim else 1 for axis in range(len(dims))])
    return factor_of


def scatter_about(own_key, dims, deviation, limit, shards=(), kind=jnp.bfloat16):
    loudness = shard_levels(own_key, dims, shards, -0.22, 0.18) if shards else 1.0
    drawn = jax.random.normal(own_key, dims, jnp.float32) * deviation * loudness
    return jnp.minimum(jnp.maximum(drawn, -limit), limit).astype(kind)


def setup_inputs(seed: int = 0) -> dict:
    streams_of = jax.random.split(jax.random.key(seed), 7)
    return {
        "query_rows": scatter_about(streams_of[0], (TOKENS, KH * DK), 1.0, 6.0, ((0, 128),)),
        "key_rows": scatter_about(streams_of[1], (TOKENS, KH * DK), 1.0, 6.0, ((0, 128),)),
        "value_rows": scatter_about(streams_of[2], (TOKENS, VH * DV), 1.0, 6.0, ((0, 128),)),
        "log_decay": draw_log_decay(jax.random.fold_in(streams_of[6], 71), 0),
        "beta_logit": draw_beta_logit(jax.random.fold_in(streams_of[6], 71), 0),
        "out_grad": scatter_about(streams_of[5], (TOKENS, VH * DV), 8.0, 48.0, ((0, 128),)),
    }


highest = lax.Precision.HIGHEST

def unit_rows(values):
    return values * lax.rsqrt(lax.optimization_barrier(jnp.sum(values * values, axis=-1, keepdims=True)) + 1e-06)

def recur(state, inputs):
    query_now, key_now, value_now, keep_now, write_now = inputs
    kept = keep_now[:, None, None] * state
    guess = jnp.einsum('rvk,k->rv', kept, key_now, precision=highest)
    update = write_now[:, None] * (value_now - guess)
    state = kept + update[:, :, None] * key_now[None, None, :]
    return (state, jnp.einsum('rvk,k->rv', state, query_now, precision=highest))

def segment(state, inputs):
    return lax.scan(recur, state, inputs)

def forward_heads(query_rows, key_rows, value_rows, log_decay, beta_logit):
    query_unit = unit_rows(query_rows) * DK ** (-0.5)
    key_unit = unit_rows(key_rows)
    keep = jnp.exp(log_decay)
    write = jax.nn.sigmoid(beta_logit)
    ratio = value_rows.shape[1]
    blocks = TOKENS // BLOCK
    inputs = tuple((item.reshape((blocks, BLOCK) + item.shape[1:]) for item in (query_unit, key_unit, value_rows, keep, write)))
    start = jnp.zeros((ratio, DV, DK), jnp.float32)
    _, result = lax.scan(jax.checkpoint(segment), start, inputs)
    return result.reshape(TOKENS, ratio, DV)

def reference(query_rows, key_rows, value_rows, log_decay, beta_logit, out_grad):
    ratio = VH // KH
    query_f = query_rows.astype(jnp.float32).reshape(TOKENS, KH, DK).transpose(1, 0, 2)
    key_f = key_rows.astype(jnp.float32).reshape(TOKENS, KH, DK).transpose(1, 0, 2)
    value_f = value_rows.astype(jnp.float32).reshape(TOKENS, KH, ratio, DV).transpose(1, 0, 2, 3)
    decay_f = log_decay.astype(jnp.float32).reshape(TOKENS, KH, ratio).transpose(1, 0, 2)
    beta_f = beta_logit.astype(jnp.float32).reshape(TOKENS, KH, ratio).transpose(1, 0, 2)
    cotangent = out_grad.astype(jnp.float32).reshape(TOKENS, KH, ratio, DV).transpose(1, 0, 2, 3)

    def one_group(inputs):
        query_one, key_one, value_one, decay_one, beta_one, cot_one = inputs
        _, pullback = jax.vjp(forward_heads, query_one, key_one, value_one, decay_one, beta_one)
        return pullback(cot_one)
    grad_q, grad_k, grad_v, grad_g, grad_b = lax.map(one_group, (query_f, key_f, value_f, decay_f, beta_f, cotangent))
    query_grad = grad_q.transpose(1, 0, 2).reshape(TOKENS, KH * DK).astype(jnp.bfloat16)
    key_grad = grad_k.transpose(1, 0, 2).reshape(TOKENS, KH * DK).astype(jnp.bfloat16)
    value_grad = grad_v.transpose(1, 0, 2, 3).reshape(TOKENS, VH * DV).astype(jnp.bfloat16)
    decay_grad = grad_g.transpose(1, 0, 2).reshape(TOKENS, VH).astype(jnp.bfloat16)
    beta_grad = grad_b.transpose(1, 0, 2).reshape(TOKENS, VH).astype(jnp.bfloat16)
    return (query_grad, key_grad, value_grad, decay_grad, beta_grad)
```

```python
import functools

import jax
import jax.numpy as jnp
from jax import lax
from jax.experimental import pallas as pl
from jax.experimental.pallas import tpu as pltpu
from jax.sharding import PartitionSpec as P

DK = 128
DV = 128
CHUNK = 128
EPS = 1e-06
QUERY_SCALE = DK ** (-0.5)

f32 = jnp.float32
bf16 = jnp.bfloat16

NN = (((1,), (0,)), ((), ()))
NT = (((1,), (1,)), ((), ()))
TN = (((0,), (0,)), ((), ()))


def dot(a, b, dims=NN):
    return lax.dot_general(a, b, dims, preferred_element_type=f32)


def low(x):
    return x.astype(bf16)


def split(x):
    high = x.astype(bf16)
    return high, (x - high.astype(f32)).astype(bf16)


def twice(a, axis):
    return jnp.concatenate([a, a], axis=axis)


def wide(x, axis):
    return jnp.concatenate(split(x), axis=axis)


def dot3(a, b, dims=NN):
    (ca,), (cb,) = dims[0]
    ah, al = split(a)
    bh, bl = split(b)
    return dot(
        jnp.concatenate([ah, al, ah], axis=ca), jnp.concatenate([bh, bh, bl], axis=cb), dims
    )


def grids(shape=(CHUNK, CHUNK)):
    return lax.broadcasted_iota(jnp.int32, shape, 0), lax.broadcasted_iota(jnp.int32, shape, 1)


def chunk_terms(pair, q, k, small):
    row, col = grids()
    causal = row >= col
    before = row > col
    eye = row == col
    key_key = dot(k, k, NT)
    query_key = dot(q, k, NT)
    qf = q.astype(f32)
    kf = k.astype(f32)
    rk_col = lax.rsqrt(jnp.sum(kf * kf, axis=1, keepdims=True) + EPS)
    rk_row = lax.rsqrt(jnp.sum(jnp.where(eye, key_key, 0.0), axis=0, keepdims=True) + EPS)
    rq_col = lax.rsqrt(jnp.sum(qf * qf, axis=1, keepdims=True) + EPS) * QUERY_SCALE
    key_key = key_key * (rk_col * rk_row)
    query_key = query_key * (rq_col * rk_row)
    lower = jnp.where(causal, 1.0, 0.0).astype(bf16)
    upper = jnp.where(row <= col, 1.0, 0.0).astype(bf16)
    ident = jnp.where(eye, 1.0, 0.0).astype(bf16)
    growth_cols = dot(lower, small)
    growth_rows = dot(small, upper, TN)
    small_rows = dot(small, ident, TN)
    small_cols = small.astype(f32)
    heads = []
    for i in range(2):
        at = 2 * pair + i
        g_col = jnp.sum(jnp.where(col == at, growth_cols, 0.0), axis=1, keepdims=True)
        g_row = jnp.sum(jnp.where(row == at, growth_rows, 0.0), axis=0, keepdims=True)
        b_col = jnp.sum(jnp.where(col == at + 8, small_cols, 0.0), axis=1, keepdims=True)
        b_row = jnp.sum(jnp.where(row == at + 8, small_rows, 0.0), axis=0, keepdims=True)
        g_end = g_col[CHUNK - 1 : CHUNK, :]
        decay = jnp.where(causal, jnp.exp(jnp.minimum(g_col - g_row, 0.0)), 0.0)
        heads.append(
            dict(
                decay=decay,
                beta_col=1.0 / (1.0 + jnp.exp(-b_col)),
                beta_row=1.0 / (1.0 + jnp.exp(-b_row)),
                growth_col=jnp.exp(g_col),
                growth_row=jnp.exp(g_row),
                to_end=jnp.exp(g_end - g_col),
                keep=jnp.exp(g_end),
            )
        )
    return dict(
        key_key=key_key,
        query_key=query_key,
        rk_col=rk_col,
        rk_row=rk_row,
        rq_col=rq_col,
        qf=qf,
        kf=kf,
        heads=heads,
    )


def inverses(systems):
    row, col = grids()
    ident = jnp.where(row == col, 1.0, 0.0)
    first = (row // 2 == col // 2) & (row > col)
    found = [ident - jnp.where(first, a, 0.0) for a in systems]
    size = 2
    while size < CHUNK:
        merge = (row // (2 * size) == col // (2 * size)) & (row // size > col // size)
        parts = [low(jnp.where(merge, a, 0.0)) for a in systems]
        lows = [low(t) for t in found]
        inner = [dot(part, t) for part, t in zip(parts, lows)]
        found = [t - dot(tl, low(x)) for t, tl, x in zip(found, lows, inner)]
        size *= 2
    rests = [ident - t - dot3(a, t) for a, t in zip(systems, found)]
    return [t + dot(low(t), low(x)) for t, x in zip(found, rests)]


def local_kernel(q_ref, k_ref, v_ref, o_ref, s_ref, send_ref, w_ref, f_ref, t_ref, u_ref, d_ref, a_ref, l_ref):
    pair = pl.program_id(0)
    row, col = grids()
    before = row > col
    chunks = q_ref.shape[0]
    terms = [chunk_terms(pair, q_ref[c], k_ref[c], s_ref[c]) for c in range(chunks)]
    systems = []
    for c in range(chunks):
        for h in terms[c]["heads"]:
            systems.append(
                jnp.where(before, h["beta_col"] * h["decay"] * terms[c]["key_key"], 0.0)
            )
    solved = inverses(systems)
    devs = [[None] * chunks, [None] * chunks]
    adds = [[None] * chunks, [None] * chunks]
    backs = [[None] * chunks, [None] * chunks]
    for c in range(chunks):
        q, k = q_ref[c], k_ref[c]
        term = terms[c]
        for i in range(2):
            h = term["heads"][i]
            t = solved[2 * c + i]
            v = v_ref[c, :, i * DV : (i + 1) * DV]
            o = o_ref[c, :, i * DV : (i + 1) * DV]
            key_part = dot(
                wide(t * (h["beta_row"] * h["growth_row"] * term["rk_row"]), 1), twice(k, 0)
            )
            value_part = dot(wide(t * h["beta_row"], 1), twice(v, 0))
            to_end = term["rk_col"] * h["to_end"]
            both = jnp.concatenate([-(to_end * key_part), to_end * value_part], axis=1)
            stepped = dot(wide(both, 0), twice(k, 0), TN)
            dev, add = stepped[:DK], stepped[DK:]
            weights = h["decay"] * term["query_key"]
            fresh = dot(wide(weights, 0), twice(o, 0), TN)
            fh, fl = split(fresh)
            wh, wl = split(key_part)
            oh, ol = split(o.astype(f32) * (h["growth_col"] * term["rq_col"]))
            back = dot(
                jnp.concatenate([oh, ol, -fh, -fl, -fh], axis=0),
                jnp.concatenate([q, q, wh, wh, wl], axis=0),
                TN,
            )
            w_ref[i, c] = key_part
            f_ref[i, c] = value_part
            t_ref[i, c] = low(t)
            u_ref[i, c] = fresh
            d_ref[i, c] = dev
            a_ref[i, c] = add
            l_ref[i, c] = back
            devs[i][c], adds[i][c], backs[i][c] = dev, add, back
    for i in range(2):
        keeps = [terms[c]["heads"][i]["keep"] for c in range(chunks)]
        stack = jnp.concatenate([devs[i][0], adds[i][0]], axis=0)
        keep = keeps[0]
        for c in range(1, chunks):
            stack = (
                keeps[c] * stack
                + dot3(stack, devs[i][c])
                + jnp.concatenate([keep * devs[i][c], adds[i][c]], axis=0)
            )
            keep = keep * keeps[c]
        grad = backs[i][chunks - 1]
        for c in reversed(range(chunks - 1)):
            grad = keeps[c] * grad + dot3(grad, devs[i][c], NT) + backs[i][c]
        dev, add = stack[:DK], stack[DK:]
        high, rest = split(keep)
        middle, last = split(keep - high.astype(f32))
        line = lax.broadcasted_iota(jnp.int32, (16, DK), 0)
        scale = low(
            jnp.where(
                line == 0,
                high.astype(f32),
                jnp.where(line == 1, middle.astype(f32), jnp.where(line == 2, last.astype(f32), 0.0)),
            )
        )
        forward, backward = low(dev), low(dev.T)
        for part in range(4):
            half = slice((part % 2) * (DV // 2), (part % 2 + 1) * (DV // 2))
            send_ref[i, part, :DK] = forward if part < 2 else backward
            send_ref[i, part, DK : DK + DV // 2] = low((add if part < 2 else grad)[half])
            send_ref[i, part, DK + DV // 2 :] = scale


def chain_kernel(order_ref, x_ref, out_ref):
    count = x_ref.shape[0]
    state = jnp.zeros((DV // 2, DK), f32)
    flip = order_ref[0]
    for step in range(count):
        at = jnp.where(flip == 1, count - 1 - step, step)
        out_ref[at] = low(state)
        if step < count - 1:
            block = x_ref[at]
            scale = jnp.sum(block[DK + DV // 2 :].astype(f32), axis=0, keepdims=True)
            state = (
                state * scale
                + dot(wide(state, 1), twice(block[:DK], 0))
                + block[DK : DK + DV // 2].astype(f32)
            )


def final_kernel(q_ref, k_ref, v_ref, o_ref, s_ref, w_ref, f_ref, t_ref, u_ref, d_ref, a_ref, l_ref, h_ref, out_ref):
    pair = pl.program_id(0)
    row, col = grids()
    before = row > col
    causal = row >= col
    suffix = jnp.where(row <= col, 1.0, 0.0).astype(bf16)
    chunks = q_ref.shape[0]
    terms = [chunk_terms(pair, q_ref[c], k_ref[c], s_ref[c]) for c in range(chunks)]
    states, grads = [], []
    for i in range(2):
        state = [h_ref[i, 0].astype(f32)]
        for c in range(chunks):
            now = state[c]
            state.append(
                terms[c]["heads"][i]["keep"] * now + dot3(now, d_ref[i, c]) + a_ref[i, c]
            )
        grad = [None] * chunks
        grad[chunks - 1] = h_ref[i, 1].astype(f32)
        for c in reversed(range(1, chunks)):
            now = grad[c]
            grad[c - 1] = (
                terms[c]["heads"][i]["keep"] * now + dot3(now, d_ref[i, c], NT) + l_ref[i, c]
            )
        states.append(state)
        grads.append(grad)

    key_heads = 4
    wide_q = key_heads * DK
    for c in range(chunks):
        q, k = q_ref[c], k_ref[c]
        term = terms[c]
        rk_col, rk_row, rq_col = term["rk_col"], term["rk_row"], term["rq_col"]
        query_unit = term["qf"] * rq_col
        key_unit = term["kf"] * rk_col
        read_sum = 0.0
        erase_sum = 0.0
        query_unit_grad = 0.0
        key_unit_grad = 0.0
        small_out = 0.0
        for i in range(2):
            h = term["heads"][i]
            o = o_ref[c, :, i * DV : (i + 1) * DV]
            state, after, grad = states[i][c], states[i][c + 1], grads[i][c]
            fresh = f_ref[i, c] - dot3(w_ref[i, c], state, NT)
            fresh_grad = u_ref[i, c] + (rk_col * h["to_end"]) * dot(
                twice(k, 1), wide(grad, 1), NT
            )
            solved = dot(twice(t_ref[i, c], 0), wide(fresh_grad, 0), TN)
            value_grad = h["beta_col"] * solved
            base = 2 * wide_q + pair * (2 * DV) + i * DV
            out_ref[c, :, pl.ds(pl.multiple_of(base, DV), DV)] = low(value_grad)
            sides = jnp.concatenate([low(value_grad), o], axis=0)
            fresh_low = low(fresh)
            inner = dot(sides, fresh_low, NT)
            outer = dot(sides, low(state))
            ended = h["to_end"] * dot(fresh_low, low(grad))
            erase = jnp.where(before, h["decay"] * inner[:CHUNK], 0.0)
            read = h["decay"] * inner[CHUNK:]
            key_read = -h["growth_col"] * outer[:CHUNK]
            query_read = h["growth_col"] * outer[CHUNK:]
            spread = read * term["query_key"] - erase * term["key_key"]
            lone = jnp.sum(
                query_unit * query_read + key_unit * (key_read - ended), axis=1, keepdims=True
            )
            lone = jnp.broadcast_to(lone, (CHUNK, CHUNK))
            sums = dot(twice(suffix, 1), wide(jnp.concatenate([spread, lone], axis=1), 0))
            decay_grad = (
                jnp.sum(jnp.where(before, sums[:, :CHUNK], 0.0), axis=1, keepdims=True)
                + sums[:, CHUNK : CHUNK + 1]
                + jnp.sum(jnp.sum(grad * after, axis=1, keepdims=True), axis=0, keepdims=True)
            )
            beta_grad = (1.0 - h["beta_col"]) * jnp.sum(solved * fresh, axis=1, keepdims=True)
            at = 2 * pair + i
            small_out = small_out + jnp.where(col == at, decay_grad, 0.0)
            small_out = small_out + jnp.where(col == at + 8, beta_grad, 0.0)
            read_sum = read_sum + read
            erase_sum = erase_sum + erase
            query_unit_grad = query_unit_grad + query_read
            key_unit_grad = key_unit_grad + key_read + ended
        query_unit_grad = query_unit_grad + dot(wide(read_sum * rk_row, 1), twice(k, 0))
        both = (erase_sum + erase_sum.T) * rk_row
        rh, rl = split((read_sum * rq_col).T)
        bh, bl = split(-both)
        key_unit_grad = key_unit_grad + dot(
            jnp.concatenate([rh, rl, bh, bl], axis=1), jnp.concatenate([q, q, k, k], axis=0)
        )
        query_back = rq_col * (
            query_unit_grad
            - query_unit
            * (DK * jnp.sum(query_unit * query_unit_grad, axis=1, keepdims=True))
        )
        key_back = rk_col * (
            key_unit_grad
            - key_unit * jnp.sum(key_unit * key_unit_grad, axis=1, keepdims=True)
        )
        out_ref[c, :, pl.ds(pl.multiple_of(pair * DK, DK), DK)] = low(query_back)
        out_ref[c, :, pl.ds(pl.multiple_of(wide_q + pair * DK, DK), DK)] = low(key_back)
        place = slice(2 * wide_q + 8 * DV, 2 * wide_q + 8 * DV + 128)
        small_out = low(small_out)
        mine = (col // 2 == pair) | (col // 2 == pair + 4)
        held = out_ref[c, :, place]
        out_ref[c, :, place] = jnp.where(mine, small_out, jnp.where(pair == 0, jnp.zeros_like(held), held))


KEY_HEADS = 4
HEADS = 8
CHUNKS = 4
SMALL_AT = 2 * KEY_HEADS * DK + 2 * HEADS * DV
IN_WIDTH = SMALL_AT + 128
OUT_WIDTH = 2 * KEY_HEADS * DK + HEADS * DV + 128
PAYLOAD = DK + DV // 2 + 16
VMEM = 56 << 20


def packed_specs():
    return [
        pl.BlockSpec((CHUNKS, CHUNK, DK), lambda p: (0, 0, p)),
        pl.BlockSpec((CHUNKS, CHUNK, DK), lambda p: (0, 0, KEY_HEADS + p)),
        pl.BlockSpec((CHUNKS, CHUNK, 2 * DV), lambda p: (0, 0, KEY_HEADS + p)),
        pl.BlockSpec((CHUNKS, CHUNK, 2 * DV), lambda p: (0, 0, 2 * KEY_HEADS + p)),
        pl.BlockSpec((CHUNKS, CHUNK, 128), lambda p: (0, 0, SMALL_AT // 128)),
    ]


SAVED = (f32, f32, bf16, f32, f32, f32, f32)


def saved_specs():
    return [pl.BlockSpec((2, CHUNKS, CHUNK, CHUNK), lambda p: (p, 0, 0, 0)) for _ in SAVED]


def local_pass(packed):
    return pl.pallas_call(
        local_kernel,
        grid=(KEY_HEADS,),
        in_specs=packed_specs(),
        out_specs=[pl.BlockSpec((2, 4, PAYLOAD, DK), lambda p: (p, 0, 0, 0))] + saved_specs(),
        out_shape=[jax.ShapeDtypeStruct((HEADS, 4, PAYLOAD, DK), bf16)]
        + [jax.ShapeDtypeStruct((HEADS, CHUNKS, CHUNK, CHUNK), kind) for kind in SAVED],
        compiler_params=pltpu.CompilerParams(vmem_limit_bytes=VMEM),
        name="local_pass",
    )(*([packed] * 5))


def chain_pass(flip, received):
    count = received.shape[0]
    return pl.pallas_call(
        chain_kernel,
        in_specs=[
            pl.BlockSpec(memory_space=pltpu.SMEM),
            pl.BlockSpec(memory_space=pltpu.VMEM),
        ],
        out_specs=pl.BlockSpec(memory_space=pltpu.VMEM),
        out_shape=jax.ShapeDtypeStruct((count, DV // 2, DK), bf16),
        compiler_params=pltpu.CompilerParams(vmem_limit_bytes=VMEM),
        name="chain_pass",
    )(flip, received)


def final_pass(packed, saved, states):
    return pl.pallas_call(
        final_kernel,
        grid=(KEY_HEADS,),
        in_specs=packed_specs()
        + saved_specs()
        + [pl.BlockSpec((2, 2, DV, DK), lambda p: (p, 0, 0, 0))],
        out_specs=pl.BlockSpec((CHUNKS, CHUNK, OUT_WIDTH), lambda p: (0, 0, 0)),
        out_shape=jax.ShapeDtypeStruct((CHUNKS, CHUNK, OUT_WIDTH), bf16),
        compiler_params=pltpu.CompilerParams(vmem_limit_bytes=VMEM),
        name="final_pass",
    )(*([packed] * 5), *saved, states)


def pack(arrays):
    split_up = [a.reshape(a.shape[0], CHUNKS, -1) for a in arrays]
    filled = sum(a.shape[2] for a in split_up)
    split_up.append(jnp.zeros((CHUNK, CHUNKS, IN_WIDTH - filled), bf16))
    return jnp.concatenate(split_up, axis=2).transpose(1, 0, 2)


def unpack(packed):
    tokens_first = packed.transpose(1, 0, 2)
    outs = []
    at = 0
    for width in (KEY_HEADS * DK, KEY_HEADS * DK, HEADS * DV, HEADS, HEADS):
        outs.append(tokens_first[:, :, at : at + width].reshape(CHUNK, -1))
        at += width
    return tuple(outs)


def on_device(query_rows, key_rows, value_rows, log_decay, beta_logit, out_grad):
    packed = lax.all_to_all(
        pack([query_rows, key_rows, value_rows, out_grad, log_decay, beta_logit]),
        "head",
        split_axis=0,
        concat_axis=0,
        tiled=True,
    )
    sends, *saved = local_pass(packed)
    segments = lax.axis_size("ctx")
    received = lax.all_to_all(
        sends.reshape(segments, PAYLOAD, DK), "ctx", split_axis=0, concat_axis=0, tiled=True
    )
    flip = (lax.axis_index("ctx") % 4 >= 2).astype(jnp.int32).reshape(1)
    chained = chain_pass(flip, received)
    states = lax.all_to_all(chained, "ctx", split_axis=0, concat_axis=0, tiled=True)
    grads = final_pass(packed, saved, states.reshape(HEADS, 2, DV, DK))
    return unpack(lax.all_to_all(grads, "head", split_axis=0, concat_axis=0, tiled=True))


def solution(mesh):
    spec = P(("ctx", "head"), None)
    return jax.shard_map(
        on_device, mesh=mesh, in_specs=(spec,) * 6, out_specs=(spec,) * 5, check_vma=False
    )
```

```python
import functools

import jax
import jax.numpy as jnp
from jax import lax
from jax.experimental import pallas as pl
from jax.experimental.pallas import tpu as pltpu
from jax.sharding import PartitionSpec as P

DK = 128
DV = 128
CHUNK = 128
EPS = 1e-06
QUERY_SCALE = DK ** (-0.5)

f32 = jnp.float32
bf16 = jnp.bfloat16

NN = (((1,), (0,)), ((), ()))
NT = (((1,), (1,)), ((), ()))
TN = (((0,), (0,)), ((), ()))


def dot(a, b, dims=NN):
    return lax.dot_general(a, b, dims, preferred_element_type=f32)


def low(x):
    return x.astype(bf16)


def split(x):
    high = x.astype(bf16)
    return high, (x - high.astype(f32)).astype(bf16)


def twice(a, axis):
    return jnp.concatenate([a, a], axis=axis)


def wide(x, axis):
    return jnp.concatenate(split(x), axis=axis)


def dot3(a, b, dims=NN):
    (ca,), (cb,) = dims[0]
    ah, al = split(a)
    bh, bl = split(b)
    return dot(
        jnp.concatenate([ah, al, ah], axis=ca), jnp.concatenate([bh, bh, bl], axis=cb), dims
    )


def grids(shape=(CHUNK, CHUNK)):
    return lax.broadcasted_iota(jnp.int32, shape, 0), lax.broadcasted_iota(jnp.int32, shape, 1)


def pickers(pair):
    row, col = grids((128, 4 * 128))
    spread = jnp.where(row == 2 * pair + (col // 128) % 2 + 8 * (col // 256), 1.0, 0.0)
    row, col = grids((32, 128))
    lines = jnp.where(col == 2 * pair + (row // 8) % 2 + 8 * (row // 16), 1.0, 0.0)
    return low(spread), low(lines)


def sigmoid(x):
    return 1.0 / (1.0 + jnp.exp(-x))


def unit_scale(x):
    return lax.rsqrt(jnp.sum(x * x, axis=1, keepdims=True) + EPS)


def chunk_terms(picks, qs, ks, smalls):
    row, col = grids()
    causal = row >= col
    eye = row == col
    spread, lines = picks
    lower = low(jnp.where(causal, 1.0, 0.0))
    upper = low(jnp.where(row <= col, 1.0, 0.0))
    key_keys = [dot(k, k, NT) for k in ks]
    query_keys = [dot(q, k, NT) for q, k in zip(qs, ks)]
    picked = [dot(small, spread) for small in smalls]
    picked_rows = [dot(lines, small, NT) for small in smalls]
    growth_cols = [dot(lower, low(x[:, :256])) for x in picked]
    growth_rows = [dot(low(x[:16]), upper) for x in picked_rows]
    terms = []
    for c in range(len(qs)):
        qf = qs[c].astype(f32)
        kf = ks[c].astype(f32)
        rk_col = unit_scale(kf)
        rk_row = lax.rsqrt(jnp.sum(jnp.where(eye, key_keys[c], 0.0), axis=0, keepdims=True) + EPS)
        rq_col = unit_scale(qf) * QUERY_SCALE
        heads = []
        for i in range(2):
            g_col = growth_cols[c][:, i * 128 : (i + 1) * 128]
            g_row = growth_rows[c][8 * i : 8 * i + 1]
            g_end = g_col[CHUNK - 1 : CHUNK, :]
            heads.append(
                dict(
                    decay=jnp.where(causal, jnp.exp(jnp.minimum(g_col - g_row, 0.0)), 0.0),
                    beta_col=sigmoid(picked[c][:, 256 + i * 128 : 384 + i * 128]),
                    beta_row=sigmoid(picked_rows[c][16 + 8 * i : 17 + 8 * i]),
                    growth_col=jnp.exp(g_col),
                    growth_row=jnp.exp(g_row),
                    to_end=jnp.exp(g_end - g_col),
                    keep=jnp.exp(g_end),
                )
            )
        terms.append(
            dict(
                key_key=key_keys[c] * (rk_col * rk_row),
                query_key=query_keys[c] * (rq_col * rk_row),
                rk_col=rk_col,
                rk_row=rk_row,
                rq_col=rq_col,
                qf=qf,
                kf=kf,
                heads=heads,
            )
        )
    return terms


def inverses(systems):
    row, col = grids()
    ident = jnp.where(row == col, 1.0, 0.0)
    first = (row // 2 == col // 2) & (row > col)
    found = [ident - jnp.where(first, a, 0.0) for a in systems]
    size = 2
    while size < CHUNK:
        merge = (row // (2 * size) == col // (2 * size)) & (row // size > col // size)
        parts = [low(jnp.where(merge, a, 0.0)) for a in systems]
        lows = [low(t) for t in found]
        inner = [dot(part, t) for part, t in zip(parts, lows)]
        found = [t - dot(tl, low(x)) for t, tl, x in zip(found, lows, inner)]
        size *= 2
    rests = [ident - t - dot3(a, t) for a, t in zip(systems, found)]
    return [t + dot(low(t), low(x)) for t, x in zip(found, rests)]


def local_kernel(base, q_ref, k_ref, v_ref, o_ref, s_ref, send_ref, w_ref, f_ref, t_ref, u_ref, d_ref, a_ref, l_ref):
    pair = base + pl.program_id(0)
    row, col = grids()
    before = row > col
    chunks = q_ref.shape[0]
    qs, ks, smalls = ([ref[c] for c in range(chunks)] for ref in (q_ref, k_ref, s_ref))
    terms = chunk_terms(pickers(pair), qs, ks, smalls)
    cases = [(c, i) for c in range(chunks) for i in range(2)]
    gates = [terms[c]["heads"][i] for c, i in cases]
    o_in = [o_ref[c, :, i * DV : (i + 1) * DV] for c, i in cases]
    v_in = [v_ref[c, :, i * DV : (i + 1) * DV] for c, i in cases]
    systems = [
        jnp.where(before, h["beta_col"] * h["decay"] * terms[c]["key_key"], 0.0)
        for (c, i), h in zip(cases, gates)
    ]
    solved = inverses(systems)
    fresh = [
        dot(wide(h["decay"] * terms[c]["query_key"], 0), twice(o, 0), TN)
        for (c, i), h, o in zip(cases, gates, o_in)
    ]
    key_part = [
        dot(wide(t * (h["beta_row"] * h["growth_row"] * terms[c]["rk_row"]), 1), twice(ks[c], 0))
        for (c, i), h, t in zip(cases, gates, solved)
    ]
    value_part = [
        dot(wide(t * h["beta_row"], 1), twice(v, 0)) for h, t, v in zip(gates, solved, v_in)
    ]
    stepped = []
    for (c, i), h, x, y in zip(cases, gates, key_part, value_part):
        to_end = terms[c]["rk_col"] * h["to_end"]
        both = jnp.concatenate([-(to_end * x), to_end * y], axis=1)
        stepped.append(dot(wide(both, 0), twice(ks[c], 0), TN))
    devs = [x[:DK] for x in stepped]
    adds = [x[DK:] for x in stepped]
    backs = []
    for (c, i), h, u, w, o in zip(cases, gates, fresh, key_part, o_in):
        fh, fl = split(u)
        wh, wl = split(w)
        oh, ol = split(o.astype(f32) * (h["growth_col"] * terms[c]["rq_col"]))
        backs.append(
            dot(
                jnp.concatenate([oh, ol, -fh, -fl, -fh], axis=0),
                jnp.concatenate([qs[c], qs[c], wh, wh, wl], axis=0),
                TN,
            )
        )
    for n, (c, i) in enumerate(cases):
        w_ref[i, c] = key_part[n]
        f_ref[i, c] = value_part[n]
        t_ref[i, c] = low(solved[n])
        u_ref[i, c] = fresh[n]
        d_ref[i, c] = devs[n]
        a_ref[i, c] = adds[n]
        l_ref[i, c] = backs[n]
    at = lambda c, i: 2 * c + i
    stacks = [jnp.concatenate([devs[i], adds[i]], axis=0) for i in range(2)]
    keeps = [gates[i]["keep"] for i in range(2)]
    grads = [backs[at(chunks - 1, i)] for i in range(2)]
    for step in range(1, chunks):
        back = chunks - 1 - step
        ahead = [dot3(stacks[i], devs[at(step, i)]) for i in range(2)]
        behind = [dot3(grads[i], devs[at(back, i)], NT) for i in range(2)]
        for i in range(2):
            n, m = at(step, i), at(back, i)
            keep = gates[n]["keep"]
            stacks[i] = (
                keep * stacks[i]
                + ahead[i]
                + jnp.concatenate([keeps[i] * devs[n], adds[n]], axis=0)
            )
            keeps[i] = keeps[i] * keep
            grads[i] = gates[m]["keep"] * grads[i] + behind[i] + backs[m]
    for i in range(2):
        dev, add = stacks[i][:DK], stacks[i][DK:]
        high, rest = split(keeps[i])
        middle, last = split(keeps[i] - high.astype(f32))
        line = lax.broadcasted_iota(jnp.int32, (16, DK), 0)
        scale = jnp.where(line == 2, last.astype(f32), 0.0)
        scale = jnp.where(line == 1, middle.astype(f32), scale)
        scale = low(jnp.where(line == 0, high.astype(f32), scale))
        forward, backward = low(dev), low(dev.T)
        for part in range(4):
            half = slice((part % 2) * (DV // 2), (part % 2 + 1) * (DV // 2))
            send_ref[i, part, :DK] = forward if part < 2 else backward
            send_ref[i, part, DK : DK + DV // 2] = low((add if part < 2 else grads[i])[half])
            send_ref[i, part, DK + DV // 2 :] = scale


def chain_kernel(flip_ref, x_ref, out_ref, state_ref):
    count = x_ref.shape[0]

    @pl.when(pl.program_id(0) == 0)
    def _():
        state_ref[...] = jnp.zeros_like(state_ref)

    state = state_ref[...]
    flip = flip_ref[0]
    for step in range(count):
        at = jnp.where(flip == 1, count - 1 - step, step)
        out_ref[at] = low(state)
        block = x_ref[at]
        scale = jnp.sum(block[DK + DV // 2 :].astype(f32), axis=0, keepdims=True)
        state = (
            state * scale
            + dot(wide(state, 1), twice(block[:DK], 0))
            + block[DK : DK + DV // 2].astype(f32)
        )
    state_ref[...] = state


def final_kernel(base, q_ref, k_ref, v_ref, o_ref, s_ref, w_ref, f_ref, t_ref, u_ref, d_ref, a_ref, l_ref, h_ref, out_ref):
    here = pl.program_id(0)
    pair = base + here
    row, col = grids()
    before = row > col
    suffix = low(jnp.where(row <= col, 1.0, 0.0))
    chunks = q_ref.shape[0]
    qs, ks, smalls = ([ref[c] for c in range(chunks)] for ref in (q_ref, k_ref, s_ref))
    terms = chunk_terms(pickers(pair), qs, ks, smalls)
    cases = [(c, i) for c in range(chunks) for i in range(2)]
    gates = [terms[c]["heads"][i] for c, i in cases]
    o_in = [o_ref[c, :, i * DV : (i + 1) * DV] for c, i in cases]

    states = [[h_ref[i, 0].astype(f32)] for i in range(2)]
    grads = [[h_ref[i, 1].astype(f32)] for i in range(2)]
    for c in range(chunks):
        back = chunks - 1 - c
        ahead = [dot3(states[i][c], d_ref[i, c]) for i in range(2)]
        if back > 0:
            behind = [dot3(grads[i][c], d_ref[i, back], NT) for i in range(2)]
        for i in range(2):
            keep = terms[c]["heads"][i]["keep"]
            states[i].append(keep * states[i][c] + ahead[i] + a_ref[i, c])
            if back > 0:
                keep = terms[back]["heads"][i]["keep"]
                grads[i].append(keep * grads[i][c] + behind[i] + l_ref[i, back])
    state_of = [states[i][c] for c, i in cases]
    after_of = [states[i][c + 1] for c, i in cases]
    grad_of = [grads[i][chunks - 1 - c] for c, i in cases]

    fresh = [
        f_ref[i, c] - dot3(w_ref[i, c], state, NT) for (c, i), state in zip(cases, state_of)
    ]
    fresh_grad = [
        u_ref[i, c]
        + (terms[c]["rk_col"] * h["to_end"]) * dot(twice(ks[c], 1), wide(grad, 1), NT)
        for (c, i), h, grad in zip(cases, gates, grad_of)
    ]
    solved = [
        dot(twice(t_ref[i, c], 0), wide(x, 0), TN) for (c, i), x in zip(cases, fresh_grad)
    ]
    value_grad = [h["beta_col"] * x for h, x in zip(gates, solved)]
    quarter = (out_ref.shape[2] - 128) // 4
    for (c, i), x in zip(cases, value_grad):
        start = 2 * quarter + here * (2 * DV) + i * DV
        out_ref[c, :, pl.ds(pl.multiple_of(start, DV), DV)] = low(x)
    sides = [jnp.concatenate([low(x), o], axis=0) for x, o in zip(value_grad, o_in)]
    fresh_low = [low(x) for x in fresh]
    outer = [dot(x, low(state)) for x, state in zip(sides, state_of)]
    ended = [
        h["to_end"] * dot(x, low(grad)) for h, x, grad in zip(gates, fresh_low, grad_of)
    ]
    inner = [dot(x, y, NT) for x, y in zip(sides, fresh_low)]
    key_read = [-h["growth_col"] * x[:CHUNK] for h, x in zip(gates, outer)]
    query_read = [h["growth_col"] * x[CHUNK:] for h, x in zip(gates, outer)]
    erase = [jnp.where(before, h["decay"] * x[:CHUNK], 0.0) for h, x in zip(gates, inner)]
    read = [h["decay"] * x[CHUNK:] for h, x in zip(gates, inner)]
    units = [(t["qf"] * t["rq_col"], t["kf"] * t["rk_col"]) for t in terms]
    sums = []
    for n, (c, i) in enumerate(cases):
        query_unit, key_unit = units[c]
        spread = read[n] * terms[c]["query_key"] - erase[n] * terms[c]["key_key"]
        lone = query_unit * query_read[n] + key_unit * (key_read[n] - ended[n])
        sums.append(dot(twice(suffix, 1), wide(jnp.concatenate([spread, lone], axis=1), 0)))
    query_inner, key_inner = [], []
    for c in range(chunks):
        term = terms[c]
        read_sum = read[2 * c] + read[2 * c + 1]
        erase_sum = erase[2 * c] + erase[2 * c + 1]
        query_inner.append(dot(wide(read_sum * term["rk_row"], 1), twice(ks[c], 0)))
        key_inner.append(
            dot(wide(erase_sum * -term["rk_row"], 1), twice(ks[c], 0))
            + dot(
                jnp.concatenate(
                    split(read_sum * term["rq_col"]) + split(erase_sum * -term["rk_col"]), axis=0
                ),
                jnp.concatenate([qs[c], qs[c], ks[c], ks[c]], axis=0),
                TN,
            )
        )
    small_out = []
    for c in range(chunks):
        parts, places = [], []
        wholes = 0.0
        for i in range(2):
            n = 2 * c + i
            at = 2 * pair + i
            for place, part in (
                (at, jnp.where(before, sums[n][:, :CHUNK], 0.0) + sums[n][:, CHUNK:]),
                (at + 8, (1.0 - gates[n]["beta_col"]) * solved[n] * fresh[n]),
            ):
                parts += split(part)
                places += [low(jnp.where(col == place, 1.0, 0.0))] * 2
            product = jnp.sum(grad_of[n] * after_of[n], axis=0, keepdims=True)
            whole = jnp.sum(product, axis=1, keepdims=True)
            wholes = wholes + jnp.where(col[:1] == at, whole, 0.0)
        small_out.append(
            dot(jnp.concatenate(parts, axis=1), jnp.concatenate(places, axis=0)) + wholes
        )
    for c in range(chunks):
        term = terms[c]
        query_unit, key_unit = units[c]
        query_grad = query_inner[c] + query_read[2 * c] + query_read[2 * c + 1]
        key_grad = (
            key_inner[c]
            + (key_read[2 * c] + ended[2 * c])
            + (key_read[2 * c + 1] + ended[2 * c + 1])
        )
        query_back = term["rq_col"] * (
            query_grad
            - query_unit * (DK * jnp.sum(query_unit * query_grad, axis=1, keepdims=True))
        )
        key_back = term["rk_col"] * (
            key_grad - key_unit * jnp.sum(key_unit * key_grad, axis=1, keepdims=True)
        )
        out_ref[c, :, pl.ds(pl.multiple_of(here * DK, DK), DK)] = low(query_back)
        out_ref[c, :, pl.ds(pl.multiple_of(quarter + here * DK, DK), DK)] = low(key_back)
        place = slice(4 * quarter, 4 * quarter + 128)
        mine = (col // 2 == pair) | (col // 2 == pair + 4)
        held = out_ref[c, :, place]
        kept = jnp.where(here == 0, jnp.zeros_like(held), held)
        out_ref[c, :, place] = jnp.where(mine, low(small_out[c]), kept)


KEY_HEADS = 4
HEADS = 8
CHUNKS = 4
GROUPS = ((0, 2), (2, 4))
PAYLOAD = DK + DV // 2 + 16
VMEM = 58 << 20


def pack_kernel(*refs):
    out_ref = refs[-1]
    at = 0
    for ref in refs[:4]:
        width = ref.shape[1]
        out_ref[0, :, at : at + width] = ref[...]
        at += width
    if len(refs) > 5:
        d_ref, b_ref = refs[4:6]
        dest = pl.program_id(0)
        row, col = grids((d_ref.shape[0], 128))
        decays = (col < HEADS) & (row == HEADS * dest + col)
        betas = (col >= HEADS) & (col < 2 * HEADS) & (row == HEADS * dest + col - HEADS)
        picks = [low(jnp.where(here, 1.0, 0.0)) for here in (decays, betas)]
        out_ref[0, :, at : at + 128] = low(
            dot(d_ref[...], picks[0], TN) + dot(b_ref[...], picks[1], TN)
        )


def pack(arrays, gates, begin, end):
    count = end - begin
    per = KEY_HEADS // count
    first = begin // count
    widths = [count * size for size in (DK, DK, 2 * DV, 2 * DV)]
    total = sum(widths) + (128 if gates else 0)
    return pl.pallas_call(
        pack_kernel,
        grid=(CHUNKS,),
        in_specs=[pl.BlockSpec((CHUNK, width), lambda j: (0, per * j + first)) for width in widths]
        + [pl.BlockSpec(gate.shape, lambda j: (0, 0)) for gate in gates],
        out_specs=pl.BlockSpec((1, CHUNK, total), lambda j: (j, 0, 0)),
        out_shape=jax.ShapeDtypeStruct((CHUNKS, CHUNK, total), bf16),
        compiler_params=pltpu.CompilerParams(vmem_limit_bytes=VMEM),
        name="pack",
    )(*arrays, *gates)


def unpack_kernel(*refs):
    groups = refs[: len(GROUPS)]
    q_ref, k_ref, v_ref, d_ref, b_ref, d_sum, b_sum = refs[len(GROUPS) :]
    source = pl.program_id(0)

    @pl.when(source == 0)
    def _():
        d_sum[...] = jnp.zeros_like(d_sum)
        b_sum[...] = jnp.zeros_like(b_sum)

    row, col = grids((d_sum.shape[0], 128))
    decays = low(jnp.where((col < HEADS) & (row == HEADS * source + col), 1.0, 0.0))
    betas = (col >= HEADS) & (col < 2 * HEADS) & (row == HEADS * source + col - HEADS)
    betas = low(jnp.where(betas, 1.0, 0.0))
    for (begin, end), ref in zip(GROUPS, groups):
        at = 0
        for out, size in ((q_ref, DK), (k_ref, DK), (v_ref, 2 * DV)):
            width = (end - begin) * size
            out[:, begin * size : end * size] = ref[0, :, at : at + width]
            at += width
        small = ref[0, :, at : at + 128]
        d_sum[...] += dot(decays, small, NT)
        b_sum[...] += dot(betas, small, NT)

    @pl.when(source == pl.num_programs(0) - 1)
    def _():
        d_ref[...] = low(d_sum[...])
        b_ref[...] = low(b_sum[...])


def unpack(groups):
    heads = CHUNKS * HEADS
    sizes = [KEY_HEADS * DK, KEY_HEADS * DK, HEADS * DV]
    q, k, v, d, b = pl.pallas_call(
        unpack_kernel,
        grid=(CHUNKS,),
        in_specs=[pl.BlockSpec((1,) + x.shape[1:], lambda j: (j, 0, 0)) for x in groups],
        out_specs=[pl.BlockSpec((CHUNK, size), lambda j: (0, j)) for size in sizes]
        + [pl.BlockSpec((heads, CHUNK), lambda j: (0, 0))] * 2,
        out_shape=[jax.ShapeDtypeStruct((CHUNK, CHUNKS * size), bf16) for size in sizes]
        + [jax.ShapeDtypeStruct((heads, CHUNK), bf16)] * 2,
        scratch_shapes=[pltpu.VMEM((heads, CHUNK), f32)] * 2,
        compiler_params=pltpu.CompilerParams(vmem_limit_bytes=VMEM),
        name="unpack",
    )(*groups)
    return q, k, v, d.T, b.T


def packed_specs(count, small_at):
    return [
        pl.BlockSpec((CHUNKS, CHUNK, DK), lambda p: (0, 0, p)),
        pl.BlockSpec((CHUNKS, CHUNK, DK), lambda p: (0, 0, count + p)),
        pl.BlockSpec((CHUNKS, CHUNK, 2 * DV), lambda p: (0, 0, count + p)),
        pl.BlockSpec((CHUNKS, CHUNK, 2 * DV), lambda p: (0, 0, 2 * count + p)),
        pl.BlockSpec((CHUNKS, CHUNK, 128), lambda p: (0, 0, small_at)),
    ]


SAVED = (f32, f32, bf16, f32, f32, f32, f32)


def saved_specs():
    return [pl.BlockSpec((2, CHUNKS, CHUNK, CHUNK), lambda p: (p, 0, 0, 0)) for _ in SAVED]


def local_pass(packed, small, small_at, begin, end, sends=None):
    count = end - begin
    kernel = functools.partial(local_kernel, begin)
    aliased = [] if sends is None else [sends]
    if aliased:
        inner = kernel
        kernel = lambda *refs: inner(*refs[:5], *refs[6:])
    return pl.pallas_call(
        kernel,
        grid=(count,),
        in_specs=packed_specs(count, small_at) + [pl.BlockSpec(memory_space=pl.ANY)] * len(aliased),
        out_specs=[pl.BlockSpec((2, 4, PAYLOAD, DK), lambda p: (begin + p, 0, 0, 0))]
        + saved_specs(),
        out_shape=[jax.ShapeDtypeStruct((HEADS, 4, PAYLOAD, DK), bf16)]
        + [jax.ShapeDtypeStruct((2 * count, CHUNKS, CHUNK, CHUNK), kind) for kind in SAVED],
        input_output_aliases={5: 0} if aliased else {},
        compiler_params=pltpu.CompilerParams(vmem_limit_bytes=VMEM),
        cost_estimate=pl.CostEstimate(
            flops=count * 4_000_000_000, bytes_accessed=count * 5_000_000, transcendentals=0
        ),
        name="local_pass",
    )(*([packed] * 4), small, *aliased)


def chain_pass(flip, received):
    count = received.shape[0]
    steps = 4
    size = count // steps
    place = lambda g, flip: (jnp.where(flip[0] == 1, steps - 1 - g, g), 0, 0)
    return pl.pallas_call(
        chain_kernel,
        grid_spec=pltpu.PrefetchScalarGridSpec(
            num_scalar_prefetch=1,
            grid=(steps,),
            in_specs=[pl.BlockSpec((size, PAYLOAD, DK), place)],
            out_specs=pl.BlockSpec((size, DV // 2, DK), place),
            scratch_shapes=[pltpu.VMEM((DV // 2, DK), f32)],
        ),
        out_shape=jax.ShapeDtypeStruct((count, DV // 2, DK), bf16),
        compiler_params=pltpu.CompilerParams(vmem_limit_bytes=VMEM),
        name="chain_pass",
    )(flip, received)


def final_pass(packed, small, small_at, saved, states, begin, end):
    count = end - begin
    width = count * 2 * (DK + DV) + 128
    return pl.pallas_call(
        functools.partial(final_kernel, begin),
        grid=(count,),
        in_specs=packed_specs(count, small_at)
        + saved_specs()
        + [pl.BlockSpec((2, 2, DV, DK), lambda p: (begin + p, 0, 0, 0))],
        out_specs=pl.BlockSpec((CHUNKS, CHUNK, width), lambda p: (0, 0, 0)),
        out_shape=jax.ShapeDtypeStruct((CHUNKS, CHUNK, width), bf16),
        compiler_params=pltpu.CompilerParams(vmem_limit_bytes=VMEM),
        cost_estimate=pl.CostEstimate(
            flops=count * 4_000_000_000, bytes_accessed=count * 5_000_000, transcendentals=0
        ),
        name="final_pass",
    )(*([packed] * 4), small, *saved, states)


def exchange(packed):
    return lax.all_to_all(packed, "head", split_axis=0, concat_axis=0, tiled=True)


def on_device(query_rows, key_rows, value_rows, log_decay, beta_logit, out_grad):
    arrays = [query_rows, key_rows, value_rows, out_grad]
    gates = [log_decay.T, beta_logit.T]
    received = [exchange(pack(arrays, gates if b == 0 else [], b, e)) for b, e in GROUPS]
    small = received[0]
    small_at = small.shape[2] // 128 - 1
    sends, saved = None, []
    for (b, e), packed in zip(GROUPS, received):
        sends, *kept = local_pass(packed, small, small_at, b, e, sends)
        saved.append(kept)
    segments = lax.axis_size("ctx")
    maps = lax.all_to_all(
        sends.reshape(segments, PAYLOAD, DK),
        "ctx",
        split_axis=0,
        concat_axis=0,
        tiled=True,
    )
    flip = (lax.axis_index("ctx") % 4 >= 2).astype(jnp.int32).reshape(1)
    states = lax.all_to_all(
        chain_pass(flip, maps), "ctx", split_axis=0, concat_axis=0, tiled=True
    ).reshape(HEADS, 2, DV, DK)
    outs = []
    for (b, e), packed, kept in zip(GROUPS, received, saved):
        outs.append(exchange(final_pass(packed, small, small_at, kept, states, b, e)))
    return unpack(outs)


def solution(mesh):
    spec = P(("ctx", "head"), None)
    return jax.shard_map(
        on_device, mesh=mesh, in_specs=(spec,) * 6, out_specs=(spec,) * 5, check_vma=False
    )
```

```python
import functools

import jax
import jax.numpy as jnp
from jax import lax
from jax.experimental import pallas as pl
from jax.experimental.pallas import tpu as pltpu
from jax.sharding import PartitionSpec as P

DK = 128
DV = 128
CHUNK = 128
EPS = 1e-06
QUERY_SCALE = DK ** (-0.5)

KEY_HEADS = 4
HEADS = 8
CHUNKS = 4
GROUPS = ((0, 2), (2, 4))
PAYLOAD = DK + DV + 16
VMEM = 58 << 20

f32 = jnp.float32
bf16 = jnp.bfloat16

NN = (((1,), (0,)), ((), ()))
NT = (((1,), (1,)), ((), ()))
TN = (((0,), (0,)), ((), ()))


def dot(a, b, dims=NN):
    return lax.dot_general(a, b, dims, preferred_element_type=f32)


def low(x):
    return x.astype(bf16)


def split(x):
    high = x.astype(bf16)
    return high, (x - high.astype(f32)).astype(bf16)


def twice(a, axis):
    return jnp.concatenate([a, a], axis=axis)


def wide(x, axis):
    return jnp.concatenate(split(x), axis=axis)


def dot3(a, b, dims=NN):
    (ca,), (cb,) = dims[0]
    ah, al = split(a)
    bh, bl = split(b)
    return dot(
        jnp.concatenate([ah, al, ah], axis=ca), jnp.concatenate([bh, bh, bl], axis=cb), dims
    )


def grids(shape=(CHUNK, CHUNK)):
    return lax.broadcasted_iota(jnp.int32, shape, 0), lax.broadcasted_iota(jnp.int32, shape, 1)


def pickers(pair):
    row, col = grids((128, 4 * 128))
    spread = jnp.where(row == 2 * pair + (col // 128) % 2 + 8 * (col // 256), 1.0, 0.0)
    row, col = grids((32, 128))
    lines = jnp.where(col == 2 * pair + (row // 8) % 2 + 8 * (row // 16), 1.0, 0.0)
    return low(spread), low(lines)


def sigmoid(x):
    return 1.0 / (1.0 + jnp.exp(-x))


def unit_scale(x):
    return lax.rsqrt(jnp.sum(x * x, axis=1, keepdims=True) + EPS)


def chunk_terms(picks, qs, ks, smalls):
    row, col = grids()
    causal = row >= col
    eye = row == col
    spread, lines = picks
    lower = low(jnp.where(causal, 1.0, 0.0))
    upper = low(jnp.where(row <= col, 1.0, 0.0))
    key_keys = [dot(k, k, NT) for k in ks]
    query_keys = [dot(q, k, NT) for q, k in zip(qs, ks)]
    picked = [dot(small, spread) for small in smalls]
    picked_rows = [dot(lines, small, NT) for small in smalls]
    growth_cols = [dot(lower, low(x[:, :256])) for x in picked]
    growth_rows = [dot(low(x[:16]), upper) for x in picked_rows]
    terms = []
    for c in range(len(qs)):
        qf = qs[c].astype(f32)
        kf = ks[c].astype(f32)
        rk_col = unit_scale(kf)
        rk_row = lax.rsqrt(jnp.sum(jnp.where(eye, key_keys[c], 0.0), axis=0, keepdims=True) + EPS)
        rq_col = unit_scale(qf) * QUERY_SCALE
        heads = []
        for i in range(2):
            g_col = growth_cols[c][:, i * 128 : (i + 1) * 128]
            g_row = growth_rows[c][8 * i : 8 * i + 1]
            g_end = g_col[CHUNK - 1 : CHUNK, :]
            heads.append(
                dict(
                    decay=jnp.where(causal, jnp.exp(jnp.minimum(g_col - g_row, 0.0)), 0.0),
                    beta_col=sigmoid(picked[c][:, 256 + i * 128 : 384 + i * 128]),
                    beta_row=sigmoid(picked_rows[c][16 + 8 * i : 17 + 8 * i]),
                    growth_col=jnp.exp(g_col),
                    growth_row=jnp.exp(g_row),
                    to_end=jnp.exp(g_end - g_col),
                    keep=jnp.exp(g_end),
                )
            )
        terms.append(
            dict(
                key_key=key_keys[c] * (rk_col * rk_row),
                query_key=query_keys[c] * (rq_col * rk_row),
                rk_col=rk_col,
                rk_row=rk_row,
                rq_col=rq_col,
                qf=qf,
                kf=kf,
                heads=heads,
            )
        )
    return terms


def inverses(systems):
    row, col = grids()
    ident = jnp.where(row == col, 1.0, 0.0)
    first = (row // 2 == col // 2) & (row > col)
    found = [ident - jnp.where(first, a, 0.0) for a in systems]
    size = 2
    while size < CHUNK:
        merge = (row // (2 * size) == col // (2 * size)) & (row // size > col // size)
        parts = [low(jnp.where(merge, a, 0.0)) for a in systems]
        lows = [low(t) for t in found]
        inner = [dot(part, t) for part, t in zip(parts, lows)]
        found = [t - dot(tl, low(x)) for t, tl, x in zip(found, lows, inner)]
        size *= 2
    rests = [ident - t - dot3(a, t) for a, t in zip(systems, found)]
    return [t + dot(low(t), low(x)) for t, x in zip(found, rests)]


def slot_of(me, chunk):
    return lax.rem(me + CHUNKS - chunk, CHUNKS)


def local_kernel(base, me_ref, *refs):
    ins, outs = refs[: 5 * CHUNKS], refs[5 * CHUNKS :]
    send_ref, w_ref, f_ref, t_ref, u_ref, d_ref, a_ref, l_ref, keep_ref = outs
    me = me_ref[0]
    pair = base + pl.program_id(0)
    row, col = grids()
    before = row > col
    chunks = CHUNKS
    qs, ks, vs, os, smalls = ([r[...] for r in ins[n * chunks : (n + 1) * chunks]] for n in range(5))
    terms = chunk_terms(pickers(pair), qs, ks, smalls)
    cases = [(c, i) for c in range(chunks) for i in range(2)]
    gates = [terms[c]["heads"][i] for c, i in cases]
    o_in = [os[c][:, i * DV : (i + 1) * DV] for c, i in cases]
    v_in = [vs[c][:, i * DV : (i + 1) * DV] for c, i in cases]
    systems = [
        jnp.where(before, h["beta_col"] * h["decay"] * terms[c]["key_key"], 0.0)
        for (c, i), h in zip(cases, gates)
    ]
    solved = inverses(systems)
    fresh = [
        dot(wide(h["decay"] * terms[c]["query_key"], 0), twice(o, 0), TN)
        for (c, i), h, o in zip(cases, gates, o_in)
    ]
    key_part = [
        dot(wide(t * (h["beta_row"] * h["growth_row"] * terms[c]["rk_row"]), 1), twice(ks[c], 0))
        for (c, i), h, t in zip(cases, gates, solved)
    ]
    value_part = [
        dot(wide(t * h["beta_row"], 1), twice(v, 0)) for h, t, v in zip(gates, solved, v_in)
    ]
    stepped = []
    for (c, i), h, x, y in zip(cases, gates, key_part, value_part):
        to_end = terms[c]["rk_col"] * h["to_end"]
        both = jnp.concatenate([-(to_end * x), to_end * y], axis=1)
        stepped.append(dot(wide(both, 0), twice(ks[c], 0), TN))
    devs = [x[:DK] for x in stepped]
    adds = [x[DK:] for x in stepped]
    backs = []
    for (c, i), h, u, w, o in zip(cases, gates, fresh, key_part, o_in):
        fh, fl = split(u)
        wh, wl = split(w)
        oh, ol = split(o.astype(f32) * (h["growth_col"] * terms[c]["rq_col"]))
        backs.append(
            dot(
                jnp.concatenate([oh, ol, -fh, -fl, -fh], axis=0),
                jnp.concatenate([qs[c], qs[c], wh, wh, wl], axis=0),
                TN,
            )
        )
    for n, (c, i) in enumerate(cases):
        w_ref[i, c] = key_part[n]
        f_ref[i, c] = value_part[n]
        t_ref[i, c] = low(solved[n])
        u_ref[i, c] = fresh[n]
        d_ref[i, c] = devs[n]
        a_ref[i, c] = adds[n]
        l_ref[i, c] = backs[n]
        keep_ref[i, c] = jnp.broadcast_to(gates[n]["keep"], (8, DK))
    first, last = slot_of(me, 0), slot_of(me, chunks - 1)
    stacks = [jnp.concatenate([d_ref[i, first], a_ref[i, first]], axis=0) for i in range(2)]
    keeps = [keep_ref[i, first][:1] for i in range(2)]
    grads = [l_ref[i, last] for i in range(2)]
    for step in range(1, chunks):
        n, m = slot_of(me, step), slot_of(me, chunks - 1 - step)
        ahead = [dot3(stacks[i], d_ref[i, n]) for i in range(2)]
        behind = [dot3(grads[i], d_ref[i, m], NT) for i in range(2)]
        for i in range(2):
            keep = keep_ref[i, n][:1]
            stacks[i] = (
                keep * stacks[i]
                + ahead[i]
                + jnp.concatenate([keeps[i] * d_ref[i, n], a_ref[i, n]], axis=0)
            )
            keeps[i] = keeps[i] * keep
            grads[i] = keep_ref[i, m][:1] * grads[i] + behind[i] + l_ref[i, m]
    for i in range(2):
        dev, add = stacks[i][:DK], stacks[i][DK:]
        high, rest = split(keeps[i])
        middle, last = split(keeps[i] - high.astype(f32))
        line = lax.broadcasted_iota(jnp.int32, (16, DK), 0)
        scale = jnp.where(line == 2, last.astype(f32), 0.0)
        scale = jnp.where(line == 1, middle.astype(f32), scale)
        scale = low(jnp.where(line == 0, high.astype(f32), scale))
        for way, (step_map, addend) in enumerate(((dev, add), (dev.T, grads[i]))):
            send_ref[i, way, :DK] = low(step_map)
            send_ref[i, way, DK : DK + DV] = low(addend)
            send_ref[i, way, DK + DV :] = scale


def segment_parts(block):
    scale = jnp.sum(block[DK + DV :].astype(f32), axis=0, keepdims=True)
    return block[:DK], block[DK : DK + DV].astype(f32), scale


def combine_kernel(where_ref, x_ref, out_ref):
    count = x_ref.shape[0]
    flip = where_ref[0]
    for step in range(count):
        at = jnp.where(flip == 1, count - 1 - step, step)
        step_map, addend, scale = segment_parts(x_ref[at])
        if step == 0:
            stack = jnp.concatenate([step_map.astype(f32), addend], axis=0)
            keep = scale
        else:
            stack = (
                scale * stack
                + dot(wide(stack, 1), twice(step_map, 0))
                + jnp.concatenate([keep * step_map.astype(f32), addend], axis=0)
            )
            keep = keep * scale
    out_ref[: DK + DV] = stack
    out_ref[DK + DV :] = jnp.broadcast_to(keep, (8, DK))


def chain_kernel(where_ref, x_ref, one_ref, two_ref, three_ref, out_ref):
    count = x_ref.shape[0]
    flip = where_ref[0]
    place = where_ref[1]
    rows = where_ref[2]
    state = jnp.zeros((DV, DK), f32)
    for n, ahead, back in ((3, three_ref, one_ref), (2, two_ref, two_ref), (1, one_ref, three_ref)):
        block = jnp.where(flip == 1, back[...], ahead[...])
        there = jnp.where(flip == 1, place + n < rows, n <= place)
        later = (
            block[DK + DV : DK + DV + 1] * state + dot3(state, block[:DK]) + block[DK : DK + DV]
        )
        state = jnp.where(there, later, state)
    for step in range(count):
        at = jnp.where(flip == 1, count - 1 - step, step)
        out_ref[at] = low(state)
        if step < count - 1:
            step_map, addend, scale = segment_parts(x_ref[at])
            state = state * scale + dot(wide(state, 1), twice(step_map, 0)) + addend


def final_kernel(base, me_ref, *refs):
    ins, refs = refs[: 5 * CHUNKS], refs[5 * CHUNKS :]
    w_ref, f_ref, t_ref, u_ref, d_ref, a_ref, l_ref, h_ref = refs[:8]
    out_refs = refs[8 : 8 + CHUNKS]
    keep_ref, state_ref, after_ref, grad_ref = refs[8 + CHUNKS :]
    me = me_ref[0]
    here = pl.program_id(0)
    pair = base + here
    row, col = grids()
    before = row > col
    suffix = low(jnp.where(row <= col, 1.0, 0.0))
    chunks = CHUNKS
    qs, ks, vs, os, smalls = ([r[...] for r in ins[n * chunks : (n + 1) * chunks]] for n in range(5))
    terms = chunk_terms(pickers(pair), qs, ks, smalls)
    cases = [(c, i) for c in range(chunks) for i in range(2)]
    gates = [terms[c]["heads"][i] for c, i in cases]
    o_in = [os[c][:, i * DV : (i + 1) * DV] for c, i in cases]

    for n, (c, i) in enumerate(cases):
        keep_ref[i, c] = jnp.broadcast_to(gates[n]["keep"], (8, DK))
    states = [h_ref[i, 0].astype(f32) for i in range(2)]
    grads = [h_ref[i, 1].astype(f32) for i in range(2)]
    for step in range(chunks):
        n, m = slot_of(me, step), slot_of(me, chunks - 1 - step)
        for i in range(2):
            state_ref[i, n] = states[i]
            grad_ref[i, m] = grads[i]
        ahead = [dot3(states[i], d_ref[i, n]) for i in range(2)]
        if step < chunks - 1:
            behind = [dot3(grads[i], d_ref[i, m], NT) for i in range(2)]
        for i in range(2):
            states[i] = keep_ref[i, n][:1] * states[i] + ahead[i] + a_ref[i, n]
            after_ref[i, n] = states[i]
            if step < chunks - 1:
                grads[i] = keep_ref[i, m][:1] * grads[i] + behind[i] + l_ref[i, m]
    state_of = [state_ref[i, c] for c, i in cases]
    after_of = [after_ref[i, c] for c, i in cases]
    grad_of = [grad_ref[i, c] for c, i in cases]

    fresh = [
        f_ref[i, c] - dot3(w_ref[i, c], state, NT) for (c, i), state in zip(cases, state_of)
    ]
    fresh_grad = [
        u_ref[i, c]
        + (terms[c]["rk_col"] * h["to_end"]) * dot(twice(ks[c], 1), wide(grad, 1), NT)
        for (c, i), h, grad in zip(cases, gates, grad_of)
    ]
    solved = [
        dot(twice(t_ref[i, c], 0), wide(x, 0), TN) for (c, i), x in zip(cases, fresh_grad)
    ]
    value_grad = [h["beta_col"] * x for h, x in zip(gates, solved)]
    quarter = (out_refs[0].shape[1] - 128) // 4
    for (c, i), x in zip(cases, value_grad):
        start = 2 * quarter + here * (2 * DV) + i * DV
        out_refs[c][:, pl.ds(pl.multiple_of(start, DV), DV)] = low(x)
    sides = [jnp.concatenate([low(x), o], axis=0) for x, o in zip(value_grad, o_in)]
    fresh_low = [low(x) for x in fresh]
    outer = [dot(x, low(state)) for x, state in zip(sides, state_of)]
    ended = [
        h["to_end"] * dot(x, low(grad)) for h, x, grad in zip(gates, fresh_low, grad_of)
    ]
    inner = [dot(x, y, NT) for x, y in zip(sides, fresh_low)]
    key_read = [-h["growth_col"] * x[:CHUNK] for h, x in zip(gates, outer)]
    query_read = [h["growth_col"] * x[CHUNK:] for h, x in zip(gates, outer)]
    erase = [jnp.where(before, h["decay"] * x[:CHUNK], 0.0) for h, x in zip(gates, inner)]
    read = [h["decay"] * x[CHUNK:] for h, x in zip(gates, inner)]
    units = [(t["qf"] * t["rq_col"], t["kf"] * t["rk_col"]) for t in terms]
    sums = []
    for n, (c, i) in enumerate(cases):
        query_unit, key_unit = units[c]
        spread = read[n] * terms[c]["query_key"] - erase[n] * terms[c]["key_key"]
        lone = query_unit * query_read[n] + key_unit * (key_read[n] - ended[n])
        sums.append(dot(twice(suffix, 1), wide(jnp.concatenate([spread, lone], axis=1), 0)))
    query_inner, key_inner = [], []
    for c in range(chunks):
        term = terms[c]
        read_sum = read[2 * c] + read[2 * c + 1]
        erase_sum = erase[2 * c] + erase[2 * c + 1]
        query_inner.append(dot(wide(read_sum * term["rk_row"], 1), twice(ks[c], 0)))
        key_inner.append(
            dot(wide(erase_sum * -term["rk_row"], 1), twice(ks[c], 0))
            + dot(
                jnp.concatenate(
                    split(read_sum * term["rq_col"]) + split(erase_sum * -term["rk_col"]), axis=0
                ),
                jnp.concatenate([qs[c], qs[c], ks[c], ks[c]], axis=0),
                TN,
            )
        )
    small_out = []
    for c in range(chunks):
        parts, places = [], []
        wholes = 0.0
        for i in range(2):
            n = 2 * c + i
            at = 2 * pair + i
            for place, part in (
                (at, jnp.where(before, sums[n][:, :CHUNK], 0.0) + sums[n][:, CHUNK:]),
                (at + 8, (1.0 - gates[n]["beta_col"]) * solved[n] * fresh[n]),
            ):
                parts += split(part)
                places += [low(jnp.where(col == place, 1.0, 0.0))] * 2
            product = jnp.sum(grad_of[n] * after_of[n], axis=0, keepdims=True)
            whole = jnp.sum(product, axis=1, keepdims=True)
            wholes = wholes + jnp.where(col[:1] == at, whole, 0.0)
        small_out.append(
            dot(jnp.concatenate(parts, axis=1), jnp.concatenate(places, axis=0)) + wholes
        )
    for c in range(chunks):
        term = terms[c]
        query_unit, key_unit = units[c]
        query_grad = query_inner[c] + query_read[2 * c] + query_read[2 * c + 1]
        key_grad = (
            key_inner[c]
            + (key_read[2 * c] + ended[2 * c])
            + (key_read[2 * c + 1] + ended[2 * c + 1])
        )
        query_back = term["rq_col"] * (
            query_grad
            - query_unit * (DK * jnp.sum(query_unit * query_grad, axis=1, keepdims=True))
        )
        key_back = term["rk_col"] * (
            key_grad - key_unit * jnp.sum(key_unit * key_grad, axis=1, keepdims=True)
        )
        out_refs[c][:, pl.ds(pl.multiple_of(here * DK, DK), DK)] = low(query_back)
        out_refs[c][:, pl.ds(pl.multiple_of(quarter + here * DK, DK), DK)] = low(key_back)
        place = slice(4 * quarter, 4 * quarter + 128)
        mine = (col // 2 == pair) | (col // 2 == pair + 4)
        held = out_refs[c][:, place]
        kept = jnp.where(here == 0, jnp.zeros_like(held), held)
        out_refs[c][:, place] = jnp.where(mine, low(small_out[c]), kept)


def pack_kernel(me_ref, *refs):
    outs = refs[-CHUNKS:]
    for slot, out_ref in enumerate(outs):
        at = 0
        for ref in refs[4 * slot : 4 * slot + 4]:
            width = ref.shape[1]
            out_ref[:, at : at + width] = ref[...]
            at += width
    if len(refs) > 5 * CHUNKS:
        d_ref, b_ref = refs[4 * CHUNKS : 4 * CHUNKS + 2]
        for slot, out_ref in enumerate(outs):
            dest = lax.rem(me_ref[0] + slot, CHUNKS)
            row, col = grids((d_ref.shape[0], 128))
            decays = (col < HEADS) & (row == HEADS * dest + col)
            betas = (col >= HEADS) & (col < 2 * HEADS) & (row == HEADS * dest + col - HEADS)
            picks = [low(jnp.where(here, 1.0, 0.0)) for here in (decays, betas)]
            out_ref[:, at : at + 128] = low(
                dot(d_ref[...], picks[0], TN) + dot(b_ref[...], picks[1], TN)
            )


def pack(me, arrays, gates, begin, end):
    count = end - begin
    per = KEY_HEADS // count
    first = begin // count
    widths = [count * size for size in (DK, DK, 2 * DV, 2 * DV)]
    total = sum(widths) + (128 if gates else 0)
    specs = []
    for slot in range(CHUNKS):
        for width in widths:
            specs.append(
                pl.BlockSpec(
                    (CHUNK, width),
                    lambda g, me, slot=slot: (0, per * lax.rem(me[0] + slot, CHUNKS) + first),
                )
            )
    return pl.pallas_call(
        pack_kernel,
        grid_spec=pltpu.PrefetchScalarGridSpec(
            num_scalar_prefetch=1,
            grid=(1,),
            in_specs=specs + [pl.BlockSpec(gate.shape, lambda g, me: (0, 0)) for gate in gates],
            out_specs=[pl.BlockSpec((CHUNK, total), lambda g, me: (0, 0))] * CHUNKS,
        ),
        out_shape=[jax.ShapeDtypeStruct((CHUNK, total), bf16)] * CHUNKS,
        compiler_params=pltpu.CompilerParams(vmem_limit_bytes=VMEM),
        name="pack",
    )(me, *(list(arrays) * CHUNKS), *gates)


def unpack_kernel(me_ref, *refs):
    arrived = refs[: len(GROUPS) * CHUNKS]
    q_ref, k_ref, v_ref, d_ref, b_ref = refs[len(GROUPS) * CHUNKS :]
    d_sum, b_sum = 0.0, 0.0
    row, col = grids((d_ref.shape[0], 128))
    for g, (begin, end) in enumerate(GROUPS):
        for slot in range(CHUNKS):
            ref = arrived[g * CHUNKS + slot]
            source = lax.rem(me_ref[0] + slot, CHUNKS)
            at = 0
            for out, size in ((q_ref, DK), (k_ref, DK), (v_ref, 2 * DV)):
                width = (end - begin) * size
                start = pl.multiple_of((source * KEY_HEADS + begin) * size, 128)
                out[:, pl.ds(start, width)] = ref[:, at : at + width]
                at += width
            small = ref[:, at : at + 128]
            decays = (col < HEADS) & (row == HEADS * source + col)
            betas = (col >= HEADS) & (col < 2 * HEADS) & (row == HEADS * source + col - HEADS)
            d_sum = d_sum + dot(low(jnp.where(decays, 1.0, 0.0)), small, NT)
            b_sum = b_sum + dot(low(jnp.where(betas, 1.0, 0.0)), small, NT)
    d_ref[...] = low(d_sum)
    b_ref[...] = low(b_sum)


def whole(shape):
    return pl.BlockSpec(shape, lambda g, me: (0,) * len(shape))


def unpack(me, groups):
    arrived = [x for group in groups for x in group]
    shapes = [(CHUNK, CHUNKS * size) for size in (KEY_HEADS * DK, KEY_HEADS * DK, HEADS * DV)]
    shapes += [(CHUNKS * HEADS, CHUNK)] * 2
    q, k, v, d, b = pl.pallas_call(
        unpack_kernel,
        grid_spec=pltpu.PrefetchScalarGridSpec(
            num_scalar_prefetch=1,
            grid=(1,),
            in_specs=[whole(x.shape) for x in arrived],
            out_specs=[whole(shape) for shape in shapes],
        ),
        out_shape=[jax.ShapeDtypeStruct(shape, bf16) for shape in shapes],
        compiler_params=pltpu.CompilerParams(vmem_limit_bytes=VMEM),
        name="unpack",
    )(me, *arrived)
    return q, k, v, d.T, b.T


def packed_specs(count, small_at):
    return (
        [pl.BlockSpec((CHUNK, DK), lambda p, me: (0, p))] * CHUNKS
        + [pl.BlockSpec((CHUNK, DK), lambda p, me: (0, count + p))] * CHUNKS
        + [pl.BlockSpec((CHUNK, 2 * DV), lambda p, me: (0, count + p))] * CHUNKS
        + [pl.BlockSpec((CHUNK, 2 * DV), lambda p, me: (0, 2 * count + p))] * CHUNKS
        + [pl.BlockSpec((CHUNK, 128), lambda p, me: (0, small_at))] * CHUNKS
    )


SAVED = (f32, f32, bf16, f32, f32, f32, f32)
SAVED_SPECS = [pl.BlockSpec((2, CHUNKS, CHUNK, CHUNK), lambda p, me: (p, 0, 0, 0)) for _ in SAVED]


def cost(count, flops):
    return pl.CostEstimate(flops=count * flops, bytes_accessed=count * 5_000_000, transcendentals=0)


def local_pass(me, packed, small, small_at, begin, end):
    count = end - begin
    return pl.pallas_call(
        functools.partial(local_kernel, begin),
        grid_spec=pltpu.PrefetchScalarGridSpec(
            num_scalar_prefetch=1,
            grid=(count,),
            in_specs=packed_specs(count, small_at),
            out_specs=[pl.BlockSpec((2, 2, PAYLOAD, DK), lambda p, me: (p, 0, 0, 0))] + SAVED_SPECS,
            scratch_shapes=[pltpu.VMEM((2, CHUNKS, 8, DK), f32)],
        ),
        out_shape=[jax.ShapeDtypeStruct((2 * count, 2, PAYLOAD, DK), bf16)]
        + [jax.ShapeDtypeStruct((2 * count, CHUNKS, CHUNK, CHUNK), kind) for kind in SAVED],
        compiler_params=pltpu.CompilerParams(vmem_limit_bytes=VMEM),
        cost_estimate=cost(count, 4_000_000_000),
        name="local_pass",
    )(me, *(list(packed) * 4), *small)


def combine_pass(place, received):
    shape = (DK + DV + 8, DK)
    return pl.pallas_call(
        combine_kernel,
        grid_spec=pltpu.PrefetchScalarGridSpec(
            num_scalar_prefetch=1,
            grid=(1,),
            in_specs=[whole(received.shape)],
            out_specs=whole(shape),
        ),
        out_shape=jax.ShapeDtypeStruct(shape, f32),
        compiler_params=pltpu.CompilerParams(vmem_limit_bytes=VMEM),
        cost_estimate=cost(1, 1_500_000_000),
        name="combine_pass",
    )(place, received)


def chain_pass(place, received, others):
    shape = (received.shape[0], DV, DK)
    return pl.pallas_call(
        chain_kernel,
        grid_spec=pltpu.PrefetchScalarGridSpec(
            num_scalar_prefetch=1,
            grid=(1,),
            in_specs=[whole(received.shape)] + [whole(x.shape) for x in others],
            out_specs=whole(shape),
        ),
        out_shape=jax.ShapeDtypeStruct(shape, bf16),
        compiler_params=pltpu.CompilerParams(vmem_limit_bytes=VMEM),
        cost_estimate=cost(1, 1_500_000_000),
        name="chain_pass",
    )(place, received, *others)


def final_pass(me, packed, small, small_at, saved, states, begin, end):
    count = end - begin
    width = count * 2 * (DK + DV) + 128
    square = (2, CHUNKS, DV, DK)
    return pl.pallas_call(
        functools.partial(final_kernel, begin),
        grid_spec=pltpu.PrefetchScalarGridSpec(
            num_scalar_prefetch=1,
            grid=(count,),
            in_specs=packed_specs(count, small_at)
            + SAVED_SPECS
            + [pl.BlockSpec((2, 2, DV, DK), lambda p, me: (p, 0, 0, 0))],
            out_specs=[pl.BlockSpec((CHUNK, width), lambda p, me: (0, 0))] * CHUNKS,
            scratch_shapes=[pltpu.VMEM((2, CHUNKS, 8, DK), f32)] + [pltpu.VMEM(square, f32)] * 3,
        ),
        out_shape=[jax.ShapeDtypeStruct((CHUNK, width), bf16)] * CHUNKS,
        compiler_params=pltpu.CompilerParams(vmem_limit_bytes=VMEM),
        cost_estimate=cost(count, 4_000_000_000),
        name="final_pass",
    )(me, *(list(packed) * 4), *small, *saved, states)


def turned(slots, way):
    count = lax.axis_size("head")
    return [slots[0]] + [
        lax.ppermute(slots[s], "head", [(i, (i + way * s) % count) for i in range(count)])
        for s in range(1, count)
    ]


def recursion(sends, place):
    segments = lax.axis_size("ctx")
    rows = segments // HEADS
    near = [[y * HEADS + r for r in range(HEADS)] for y in range(rows)]
    received = lax.all_to_all(
        sends, "ctx", split_axis=0, concat_axis=0, axis_index_groups=near, tiled=True
    )
    combined = combine_pass(place, received)
    others = [
        lax.ppermute(
            combined, "ctx", [(i, (i + s * HEADS) % segments) for i in range(segments)]
        )
        for s in range(1, rows)
    ]
    return lax.all_to_all(
        chain_pass(place, received, others),
        "ctx",
        split_axis=0,
        concat_axis=0,
        axis_index_groups=near,
        tiled=True,
    )


def on_device(query_rows, key_rows, value_rows, log_decay, beta_logit, out_grad):
    arrays = [query_rows, key_rows, value_rows, out_grad]
    gates = [log_decay.T, beta_logit.T]
    me = lax.axis_index("head").astype(jnp.int32).reshape(1)
    segment = lax.axis_index("ctx").astype(jnp.int32)
    rows = lax.axis_size("ctx") // HEADS
    place = jnp.stack([segment % 2, segment // HEADS, jnp.int32(rows)])
    received = []
    for b, e in GROUPS:
        slots = pack(me, arrays, gates if b == 0 else [], b, e)
        if received:
            slots, received[-1] = lax.optimization_barrier((slots, received[-1]))
        received.append(turned(slots, 1))
    small = received[0]
    small_at = small[0].shape[1] // 128 - 1
    saved, states, outs = [], [], []
    for (b, e), packed in zip(GROUPS, received):
        sends, *kept = local_pass(me, packed, small, small_at, b, e)
        saved.append(kept)
        found = recursion(sends.reshape(HEADS, PAYLOAD, DK), place)
        states.append(found.reshape(2 * (e - b), 2, DV, DK))
    for (b, e), packed, kept, state in zip(GROUPS, received, saved, states):
        outs.append(turned(final_pass(me, packed, small, small_at, kept, state, b, e), -1))
    return unpack(me, outs)


def solution(mesh):
    spec = P(("ctx", "head"), None)
    return jax.shard_map(
        on_device, mesh=mesh, in_specs=(spec,) * 6, out_specs=(spec,) * 5, check_vma=False
    )
```

```python
import functools

import jax
import jax.numpy as jnp
from jax import lax
from jax.experimental import pallas as pl
from jax.experimental.pallas import tpu as pltpu
from jax.sharding import PartitionSpec as P

DK = 128
DV = 128
CHUNK = 128
EPS = 1e-06
QUERY_SCALE = DK ** (-0.5)

KEY_HEADS = 4
HEADS = 8
CHUNKS = 4
GROUPS = ((0, 2), (2, 4))
PAYLOAD = DK + DV + 16
VMEM = 64 << 20

f32 = jnp.float32
bf16 = jnp.bfloat16

NN = (((1,), (0,)), ((), ()))
NT = (((1,), (1,)), ((), ()))
TN = (((0,), (0,)), ((), ()))


def dot(a, b, dims=NN):
    return lax.dot_general(a, b, dims, preferred_element_type=f32)


def low(x):
    return x.astype(bf16)


def split(x):
    high = x.astype(bf16)
    return high, (x - high.astype(f32)).astype(bf16)


def twice(a, axis):
    return jnp.concatenate([a, a], axis=axis)


def wide(x, axis):
    return jnp.concatenate(split(x), axis=axis)


def dot3(a, b, dims=NN):
    (ca,), (cb,) = dims[0]
    ah, al = split(a)
    bh, bl = split(b)
    return dot(
        jnp.concatenate([ah, al, ah], axis=ca), jnp.concatenate([bh, bh, bl], axis=cb), dims
    )


def grids(shape=(CHUNK, CHUNK)):
    return lax.broadcasted_iota(jnp.int32, shape, 0), lax.broadcasted_iota(jnp.int32, shape, 1)


def pickers(pair):
    row, col = grids((128, 4 * 128))
    spread = jnp.where(row == 2 * pair + (col // 128) % 2 + 8 * (col // 256), 1.0, 0.0)
    row, col = grids((32, 128))
    lines = jnp.where(col == 2 * pair + (row // 8) % 2 + 8 * (row // 16), 1.0, 0.0)
    return low(spread), low(lines)


def sigmoid(x):
    return 1.0 / (1.0 + jnp.exp(-x))


def unit_scale(x):
    return lax.rsqrt(jnp.sum(x * x, axis=1, keepdims=True) + EPS)


def chunk_terms(picks, qs, ks, smalls):
    row, col = grids()
    causal = row >= col
    eye = row == col
    spread, lines = picks
    lower = low(jnp.where(causal, 1.0, 0.0))
    upper = low(jnp.where(row <= col, 1.0, 0.0))
    key_keys = [dot(k, k, NT) for k in ks]
    query_keys = [dot(q, k, NT) for q, k in zip(qs, ks)]
    picked = [dot(small, spread) for small in smalls]
    picked_rows = [dot(lines, small, NT) for small in smalls]
    growth_cols = [dot(lower, low(x[:, :256])) for x in picked]
    growth_rows = [dot(low(x[:16]), upper) for x in picked_rows]
    terms = []
    for c in range(len(qs)):
        qf = qs[c].astype(f32)
        kf = ks[c].astype(f32)
        rk_col = unit_scale(kf)
        rk_row = lax.rsqrt(jnp.sum(jnp.where(eye, key_keys[c], 0.0), axis=0, keepdims=True) + EPS)
        rq_col = unit_scale(qf) * QUERY_SCALE
        heads = []
        for i in range(2):
            g_col = growth_cols[c][:, i * 128 : (i + 1) * 128]
            g_row = growth_rows[c][8 * i : 8 * i + 1]
            g_end = g_col[CHUNK - 1 : CHUNK, :]
            heads.append(
                dict(
                    decay=jnp.where(causal, jnp.exp(jnp.minimum(g_col - g_row, 0.0)), 0.0),
                    beta_col=sigmoid(picked[c][:, 256 + i * 128 : 384 + i * 128]),
                    beta_row=sigmoid(picked_rows[c][16 + 8 * i : 17 + 8 * i]),
                    growth_col=jnp.exp(g_col),
                    growth_row=jnp.exp(g_row),
                    to_end=jnp.exp(g_end - g_col),
                    keep=jnp.exp(g_end),
                )
            )
        terms.append(
            dict(
                key_key=key_keys[c] * (rk_col * rk_row),
                query_key=query_keys[c] * (rq_col * rk_row),
                rk_col=rk_col,
                rk_row=rk_row,
                rq_col=rq_col,
                qf=qf,
                kf=kf,
                heads=heads,
            )
        )
    return terms


def inverses(systems):
    row, col = grids()
    ident = jnp.where(row == col, 1.0, 0.0)
    first = (row // 2 == col // 2) & (row > col)
    found = [ident - jnp.where(first, a, 0.0) for a in systems]
    size = 2
    while size < CHUNK:
        merge = (row // (2 * size) == col // (2 * size)) & (row // size > col // size)
        parts = [low(jnp.where(merge, a, 0.0)) for a in systems]
        lows = [low(t) for t in found]
        inner = [dot(part, t) for part, t in zip(parts, lows)]
        found = [t - dot(tl, low(x)) for t, tl, x in zip(found, lows, inner)]
        size *= 2
    rests = [ident - t - dot3(a, t) for a, t in zip(systems, found)]
    return [t + dot(low(t), low(x)) for t, x in zip(found, rests)]


def slot_of(me, chunk):
    return lax.rem(me + CHUNKS - chunk, CHUNKS)


def in_order(me, slots):
    ordered = []
    for chunk in range(CHUNKS):
        found = slots[0]
        for slot in range(1, CHUNKS):
            found = jnp.where(lax.rem(me + CHUNKS - slot, CHUNKS) == chunk, slots[slot], found)
        ordered.append(found)
    return ordered


def slot_of(me, chunk):
    return lax.rem(me + CHUNKS - chunk, CHUNKS)


def inputs_of(me, refs):
    return [in_order(me, [r[...] for r in refs[n * CHUNKS : (n + 1) * CHUNKS]]) for n in range(5)]


def local_kernel(base, me_ref, *refs):
    ins, outs = refs[: 5 * CHUNKS], refs[5 * CHUNKS :]
    send_ref, w_ref, f_ref, t_ref, u_ref, d_ref, a_ref, l_ref = outs
    me = me_ref[0]
    pair = base + pl.program_id(0)
    row, col = grids()
    before = row > col
    chunks = CHUNKS
    qs, ks, vs, os, smalls = inputs_of(me, ins)
    terms = chunk_terms(pickers(pair), qs, ks, smalls)
    cases = [(c, i) for c in range(chunks) for i in range(2)]
    gates = [terms[c]["heads"][i] for c, i in cases]
    o_in = [os[c][:, i * DV : (i + 1) * DV] for c, i in cases]
    v_in = [vs[c][:, i * DV : (i + 1) * DV] for c, i in cases]
    systems = [
        jnp.where(before, h["beta_col"] * h["decay"] * terms[c]["key_key"], 0.0)
        for (c, i), h in zip(cases, gates)
    ]
    solved = inverses(systems)
    fresh = [
        dot(wide(h["decay"] * terms[c]["query_key"], 0), twice(o, 0), TN)
        for (c, i), h, o in zip(cases, gates, o_in)
    ]
    key_part = [
        dot(wide(t * (h["beta_row"] * h["growth_row"] * terms[c]["rk_row"]), 1), twice(ks[c], 0))
        for (c, i), h, t in zip(cases, gates, solved)
    ]
    value_part = [
        dot(wide(t * h["beta_row"], 1), twice(v, 0)) for h, t, v in zip(gates, solved, v_in)
    ]
    stepped = []
    for (c, i), h, x, y in zip(cases, gates, key_part, value_part):
        to_end = terms[c]["rk_col"] * h["to_end"]
        both = jnp.concatenate([-(to_end * x), to_end * y], axis=1)
        stepped.append(dot(wide(both, 0), twice(ks[c], 0), TN))
    devs = [x[:DK] for x in stepped]
    adds = [x[DK:] for x in stepped]
    backs = []
    for (c, i), h, u, w, o in zip(cases, gates, fresh, key_part, o_in):
        fh, fl = split(u)
        wh, wl = split(w)
        oh, ol = split(o.astype(f32) * (h["growth_col"] * terms[c]["rq_col"]))
        backs.append(
            dot(
                jnp.concatenate([oh, ol, -fh, -fl, -fh], axis=0),
                jnp.concatenate([qs[c], qs[c], wh, wh, wl], axis=0),
                TN,
            )
        )
    for n, (c, i) in enumerate(cases):
        slot = slot_of(me, c)
        w_ref[i, slot] = key_part[n]
        f_ref[i, slot] = value_part[n]
        t_ref[i, slot] = low(solved[n])
        u_ref[i, slot] = fresh[n]
        d_ref[i, slot] = devs[n]
        a_ref[i, slot] = adds[n]
        l_ref[i, slot] = backs[n]
    at = lambda c, i: 2 * c + i
    stacks = [jnp.concatenate([devs[i], adds[i]], axis=0) for i in range(2)]
    keeps = [gates[i]["keep"] for i in range(2)]
    grads = [backs[at(chunks - 1, i)] for i in range(2)]
    for step in range(1, chunks):
        back = chunks - 1 - step
        ahead = [dot3(stacks[i], devs[at(step, i)]) for i in range(2)]
        behind = [dot3(grads[i], devs[at(back, i)], NT) for i in range(2)]
        for i in range(2):
            n, m = at(step, i), at(back, i)
            keep = gates[n]["keep"]
            stacks[i] = (
                keep * stacks[i]
                + ahead[i]
                + jnp.concatenate([keeps[i] * devs[n], adds[n]], axis=0)
            )
            keeps[i] = keeps[i] * keep
            grads[i] = gates[m]["keep"] * grads[i] + behind[i] + backs[m]
    for i in range(2):
        high, rest = split(keeps[i])
        middle, last = split(keeps[i] - high.astype(f32))
        line = lax.broadcasted_iota(jnp.int32, (16, DK), 0)
        scale = jnp.where(line == 2, last.astype(f32), 0.0)
        scale = jnp.where(line == 1, middle.astype(f32), scale)
        scale = low(jnp.where(line == 0, high.astype(f32), scale))
        dev, add = stacks[i][:DK], stacks[i][DK:]
        for way, (step_map, addend) in enumerate(((dev, add), (dev.T, grads[i]))):
            send_ref[i, way, :DK] = low(step_map)
            send_ref[i, way, DK : DK + DV] = low(addend)
            send_ref[i, way, DK + DV :] = scale


def segment_parts(block):
    scale = jnp.sum(block[DK + DV :].astype(f32), axis=0, keepdims=True)
    return block[:DK], block[DK : DK + DV].astype(f32), scale


def combine_kernel(where_ref, x_ref, out_ref, before_ref):
    count = x_ref.shape[0]
    flip = where_ref[0]
    stack = jnp.zeros((DK + DV, DK), f32)
    keep = jnp.ones((1, DK), f32)
    for step in range(count):
        at = jnp.where(flip == 1, count - 1 - step, step)
        before_ref[at, : DK + DV] = stack
        before_ref[at, DK + DV :] = jnp.broadcast_to(keep, (8, DK))
        step_map, addend, scale = segment_parts(x_ref[at])
        new = jnp.concatenate([keep * step_map.astype(f32), addend], axis=0)
        if step > 0:
            new = new + scale * stack + dot(wide(stack, 1), twice(step_map, 0))
        stack = new
        keep = keep * scale
    out_ref[: DK + DV] = stack
    out_ref[DK + DV :] = jnp.broadcast_to(keep, (8, DK))


def chain_kernel(where_ref, before_ref, one_ref, two_ref, three_ref, out_ref):
    flip = where_ref[0]
    place = where_ref[1]
    rows = where_ref[2]
    state = jnp.zeros((DV, DK), f32)
    for n, ahead, back in ((3, three_ref, one_ref), (2, two_ref, two_ref), (1, one_ref, three_ref)):
        block = jnp.where(flip == 1, back[...], ahead[...])
        there = jnp.where(flip == 1, place + n < rows, n <= place)
        later = block[DK + DV : DK + DV + 1] * state + block[DK : DK + DV]
        if n < 3:
            later = later + dot3(state, block[:DK])
        state = jnp.where(there, later, state)
    for step in range(before_ref.shape[0]):
        keep = before_ref[step, DK + DV : DK + DV + 1]
        met = dot3(state, before_ref[step, :DK])
        out_ref[step] = low(keep * state + met + before_ref[step, DK : DK + DV])


def final_kernel(base, me_ref, *refs):
    ins, refs = refs[: 5 * CHUNKS], refs[5 * CHUNKS :]
    w_ref, f_ref, t_ref, u_ref, d_ref, a_ref, l_ref, h_ref = refs[:8]
    out_refs = refs[8 : 8 + CHUNKS]
    keep_ref, state_ref, after_ref, grad_ref = refs[8 + CHUNKS :]
    me = me_ref[0]
    here = pl.program_id(0)
    pair = base + here
    row, col = grids()
    before = row > col
    suffix = low(jnp.where(row <= col, 1.0, 0.0))
    chunks = CHUNKS
    qs, ks, vs, os, smalls = ([r[...] for r in ins[n * chunks : (n + 1) * chunks]] for n in range(5))
    terms = chunk_terms(pickers(pair), qs, ks, smalls)
    cases = [(c, i) for c in range(chunks) for i in range(2)]
    gates = [terms[c]["heads"][i] for c, i in cases]
    o_in = [os[c][:, i * DV : (i + 1) * DV] for c, i in cases]

    for n, (c, i) in enumerate(cases):
        keep_ref[i, c] = jnp.broadcast_to(gates[n]["keep"], (8, DK))
    states = [h_ref[i, 0].astype(f32) for i in range(2)]
    grads = [h_ref[i, 1].astype(f32) for i in range(2)]
    for step in range(chunks):
        n, m = slot_of(me, step), slot_of(me, chunks - 1 - step)
        for i in range(2):
            state_ref[i, n] = states[i]
            grad_ref[i, m] = grads[i]
        ahead = [dot3(states[i], d_ref[i, n]) for i in range(2)]
        if step < chunks - 1:
            behind = [dot3(grads[i], d_ref[i, m], NT) for i in range(2)]
        for i in range(2):
            states[i] = keep_ref[i, n][:1] * states[i] + ahead[i] + a_ref[i, n]
            after_ref[i, n] = states[i]
            if step < chunks - 1:
                grads[i] = keep_ref[i, m][:1] * grads[i] + behind[i] + l_ref[i, m]
    state_of = [state_ref[i, c] for c, i in cases]
    after_of = [after_ref[i, c] for c, i in cases]
    grad_of = [grad_ref[i, c] for c, i in cases]

    fresh = [
        f_ref[i, c] - dot3(w_ref[i, c], state, NT) for (c, i), state in zip(cases, state_of)
    ]
    fresh_grad = [
        u_ref[i, c]
        + (terms[c]["rk_col"] * h["to_end"]) * dot(twice(ks[c], 1), wide(grad, 1), NT)
        for (c, i), h, grad in zip(cases, gates, grad_of)
    ]
    solved = [
        dot(twice(t_ref[i, c], 0), wide(x, 0), TN) for (c, i), x in zip(cases, fresh_grad)
    ]
    value_grad = [h["beta_col"] * x for h, x in zip(gates, solved)]
    quarter = (out_refs[0].shape[1] - 128) // 4
    for (c, i), x in zip(cases, value_grad):
        start = 2 * quarter + here * (2 * DV) + i * DV
        out_refs[c][:, pl.ds(pl.multiple_of(start, DV), DV)] = low(x)
    sides = [jnp.concatenate([low(x), o], axis=0) for x, o in zip(value_grad, o_in)]
    fresh_low = [low(x) for x in fresh]
    outer = [dot(x, low(state)) for x, state in zip(sides, state_of)]
    ended = [
        h["to_end"] * dot(x, low(grad)) for h, x, grad in zip(gates, fresh_low, grad_of)
    ]
    inner = [dot(x, y, NT) for x, y in zip(sides, fresh_low)]
    key_read = [-h["growth_col"] * x[:CHUNK] for h, x in zip(gates, outer)]
    query_read = [h["growth_col"] * x[CHUNK:] for h, x in zip(gates, outer)]
    erase = [jnp.where(before, h["decay"] * x[:CHUNK], 0.0) for h, x in zip(gates, inner)]
    read = [h["decay"] * x[CHUNK:] for h, x in zip(gates, inner)]
    units = [(t["qf"] * t["rq_col"], t["kf"] * t["rk_col"]) for t in terms]
    sums = []
    for n, (c, i) in enumerate(cases):
        query_unit, key_unit = units[c]
        spread = read[n] * terms[c]["query_key"] - erase[n] * terms[c]["key_key"]
        lone = query_unit * query_read[n] + key_unit * (key_read[n] - ended[n])
        sums.append(dot(twice(suffix, 1), wide(jnp.concatenate([spread, lone], axis=1), 0)))
    query_inner, key_inner = [], []
    for c in range(chunks):
        term = terms[c]
        read_sum = read[2 * c] + read[2 * c + 1]
        erase_sum = erase[2 * c] + erase[2 * c + 1]
        query_inner.append(dot(wide(read_sum * term["rk_row"], 1), twice(ks[c], 0)))
        key_inner.append(
            dot(wide(erase_sum * -term["rk_row"], 1), twice(ks[c], 0))
            + dot(
                jnp.concatenate(
                    split(read_sum * term["rq_col"]) + split(erase_sum * -term["rk_col"]), axis=0
                ),
                jnp.concatenate([qs[c], qs[c], ks[c], ks[c]], axis=0),
                TN,
            )
        )
    small_out = []
    for c in range(chunks):
        parts, places = [], []
        wholes = 0.0
        for i in range(2):
            n = 2 * c + i
            at = 2 * pair + i
            for place, part in (
                (at, jnp.where(before, sums[n][:, :CHUNK], 0.0) + sums[n][:, CHUNK:]),
                (at + 8, (1.0 - gates[n]["beta_col"]) * solved[n] * fresh[n]),
            ):
                parts += split(part)
                places += [low(jnp.where(col == place, 1.0, 0.0))] * 2
            product = jnp.sum(grad_of[n] * after_of[n], axis=0, keepdims=True)
            whole = jnp.sum(product, axis=1, keepdims=True)
            wholes = wholes + jnp.where(col[:1] == at, whole, 0.0)
        small_out.append(
            dot(jnp.concatenate(parts, axis=1), jnp.concatenate(places, axis=0)) + wholes
        )
    for c in range(chunks):
        term = terms[c]
        query_unit, key_unit = units[c]
        query_grad = query_inner[c] + query_read[2 * c] + query_read[2 * c + 1]
        key_grad = (
            key_inner[c]
            + (key_read[2 * c] + ended[2 * c])
            + (key_read[2 * c + 1] + ended[2 * c + 1])
        )
        query_back = term["rq_col"] * (
            query_grad
            - query_unit * (DK * jnp.sum(query_unit * query_grad, axis=1, keepdims=True))
        )
        key_back = term["rk_col"] * (
            key_grad - key_unit * jnp.sum(key_unit * key_grad, axis=1, keepdims=True)
        )
        out_refs[c][:, pl.ds(pl.multiple_of(here * DK, DK), DK)] = low(query_back)
        out_refs[c][:, pl.ds(pl.multiple_of(quarter + here * DK, DK), DK)] = low(key_back)
        place = slice(4 * quarter, 4 * quarter + 128)
        mine = (col // 2 == pair) | (col // 2 == pair + 4)
        held = out_refs[c][:, place]
        kept = jnp.where(here == 0, jnp.zeros_like(held), held)
        out_refs[c][:, place] = jnp.where(mine, low(small_out[c]), kept)


def pack_kernel(me_ref, *refs):
    outs = refs[-CHUNKS:]
    for slot, out_ref in enumerate(outs):
        at = 0
        for ref in refs[4 * slot : 4 * slot + 4]:
            width = ref.shape[1]
            out_ref[:, at : at + width] = ref[...]
            at += width
    if len(refs) > 5 * CHUNKS:
        d_ref, b_ref = refs[4 * CHUNKS : 4 * CHUNKS + 2]
        for slot, out_ref in enumerate(outs):
            dest = lax.rem(me_ref[0] + slot, CHUNKS)
            row, col = grids((d_ref.shape[0], 128))
            decays = (col < HEADS) & (row == HEADS * dest + col)
            betas = (col >= HEADS) & (col < 2 * HEADS) & (row == HEADS * dest + col - HEADS)
            picks = [low(jnp.where(here, 1.0, 0.0)) for here in (decays, betas)]
            out_ref[:, at : at + 128] = low(
                dot(d_ref[...], picks[0], TN) + dot(b_ref[...], picks[1], TN)
            )


def pack(me, arrays, gates, begin, end):
    count = end - begin
    per = KEY_HEADS // count
    first = begin // count
    widths = [count * size for size in (DK, DK, 2 * DV, 2 * DV)]
    total = sum(widths) + (128 if gates else 0)
    specs = []
    for slot in range(CHUNKS):
        for width in widths:
            specs.append(
                pl.BlockSpec(
                    (CHUNK, width),
                    lambda g, me, slot=slot: (0, per * lax.rem(me[0] + slot, CHUNKS) + first),
                )
            )
    return pl.pallas_call(
        pack_kernel,
        grid_spec=pltpu.PrefetchScalarGridSpec(
            num_scalar_prefetch=1,
            grid=(1,),
            in_specs=specs + [pl.BlockSpec(gate.shape, lambda g, me: (0, 0)) for gate in gates],
            out_specs=[pl.BlockSpec((CHUNK, total), lambda g, me: (0, 0))] * CHUNKS,
        ),
        out_shape=[jax.ShapeDtypeStruct((CHUNK, total), bf16)] * CHUNKS,
        compiler_params=pltpu.CompilerParams(vmem_limit_bytes=VMEM),
        name="pack",
    )(me, *(list(arrays) * CHUNKS), *gates)


def unpack_kernel(me_ref, *refs):
    arrived = refs[: len(GROUPS) * CHUNKS]
    q_ref, k_ref, v_ref, d_ref, b_ref = refs[len(GROUPS) * CHUNKS :]
    d_sum, b_sum = 0.0, 0.0
    row, col = grids((d_ref.shape[0], 128))
    for g, (begin, end) in enumerate(GROUPS):
        for slot in range(CHUNKS):
            ref = arrived[g * CHUNKS + slot]
            source = lax.rem(me_ref[0] + slot, CHUNKS)
            at = 0
            for out, size in ((q_ref, DK), (k_ref, DK), (v_ref, 2 * DV)):
                width = (end - begin) * size
                start = pl.multiple_of((source * KEY_HEADS + begin) * size, 128)
                out[:, pl.ds(start, width)] = ref[:, at : at + width]
                at += width
            small = ref[:, at : at + 128]
            decays = (col < HEADS) & (row == HEADS * source + col)
            betas = (col >= HEADS) & (col < 2 * HEADS) & (row == HEADS * source + col - HEADS)
            d_sum = d_sum + dot(low(jnp.where(decays, 1.0, 0.0)), small, NT)
            b_sum = b_sum + dot(low(jnp.where(betas, 1.0, 0.0)), small, NT)
    d_ref[...] = low(d_sum)
    b_ref[...] = low(b_sum)


def whole(shape):
    return pl.BlockSpec(shape, lambda g, me: (0,) * len(shape))


def unpack(me, groups):
    arrived = [x for group in groups for x in group]
    shapes = [(CHUNK, CHUNKS * size) for size in (KEY_HEADS * DK, KEY_HEADS * DK, HEADS * DV)]
    shapes += [(CHUNKS * HEADS, CHUNK)] * 2
    q, k, v, d, b = pl.pallas_call(
        unpack_kernel,
        grid_spec=pltpu.PrefetchScalarGridSpec(
            num_scalar_prefetch=1,
            grid=(1,),
            in_specs=[whole(x.shape) for x in arrived],
            out_specs=[whole(shape) for shape in shapes],
        ),
        out_shape=[jax.ShapeDtypeStruct(shape, bf16) for shape in shapes],
        compiler_params=pltpu.CompilerParams(vmem_limit_bytes=VMEM),
        name="unpack",
    )(me, *arrived)
    return q, k, v, d.T, b.T


def packed_specs(count, small_at):
    return (
        [pl.BlockSpec((CHUNK, DK), lambda p, me: (0, p))] * CHUNKS
        + [pl.BlockSpec((CHUNK, DK), lambda p, me: (0, count + p))] * CHUNKS
        + [pl.BlockSpec((CHUNK, 2 * DV), lambda p, me: (0, count + p))] * CHUNKS
        + [pl.BlockSpec((CHUNK, 2 * DV), lambda p, me: (0, 2 * count + p))] * CHUNKS
        + [pl.BlockSpec((CHUNK, 128), lambda p, me: (0, small_at))] * CHUNKS
    )


SAVED = (f32, f32, bf16, f32, f32, f32, f32)
SAVED_SPECS = [pl.BlockSpec((2, CHUNKS, CHUNK, CHUNK), lambda p, me: (p, 0, 0, 0)) for _ in SAVED]


def cost(count, flops):
    return pl.CostEstimate(flops=count * flops, bytes_accessed=count * 5_000_000, transcendentals=0)


def local_pass(me, packed, small, small_at, begin, end):
    count = end - begin
    return pl.pallas_call(
        functools.partial(local_kernel, begin),
        grid_spec=pltpu.PrefetchScalarGridSpec(
            num_scalar_prefetch=1,
            grid=(count,),
            in_specs=packed_specs(count, small_at),
            out_specs=[pl.BlockSpec((2, 2, PAYLOAD, DK), lambda p, me: (p, 0, 0, 0))] + SAVED_SPECS,
        ),
        out_shape=[jax.ShapeDtypeStruct((2 * count, 2, PAYLOAD, DK), bf16)]
        + [jax.ShapeDtypeStruct((2 * count, CHUNKS, CHUNK, CHUNK), kind) for kind in SAVED],
        compiler_params=pltpu.CompilerParams(vmem_limit_bytes=VMEM),
        cost_estimate=cost(count, 4_000_000_000),
        name="local_pass",
    )(me, *(list(packed) * 4), *small)


def combine_pass(place, received):
    shape = (DK + DV + 8, DK)
    each = (received.shape[0],) + shape
    return pl.pallas_call(
        combine_kernel,
        grid_spec=pltpu.PrefetchScalarGridSpec(
            num_scalar_prefetch=1,
            grid=(1,),
            in_specs=[whole(received.shape)],
            out_specs=[whole(shape), whole(each)],
        ),
        out_shape=[jax.ShapeDtypeStruct(shape, f32), jax.ShapeDtypeStruct(each, f32)],
        compiler_params=pltpu.CompilerParams(vmem_limit_bytes=VMEM),
        cost_estimate=cost(1, 1_500_000_000),
        name="combine_pass",
    )(place, received)


def chain_pass(place, before, others):
    shape = (before.shape[0], DV, DK)
    return pl.pallas_call(
        chain_kernel,
        grid_spec=pltpu.PrefetchScalarGridSpec(
            num_scalar_prefetch=1,
            grid=(1,),
            in_specs=[whole(before.shape)] + [whole(x.shape) for x in others],
            out_specs=whole(shape),
        ),
        out_shape=jax.ShapeDtypeStruct(shape, bf16),
        compiler_params=pltpu.CompilerParams(vmem_limit_bytes=VMEM),
        cost_estimate=cost(1, 1_500_000_000),
        name="chain_pass",
    )(place, before, *others)


def final_pass(me, packed, small, small_at, saved, states, begin, end):
    count = end - begin
    width = count * 2 * (DK + DV) + 128
    square = (2, CHUNKS, DV, DK)
    return pl.pallas_call(
        functools.partial(final_kernel, begin),
        grid_spec=pltpu.PrefetchScalarGridSpec(
            num_scalar_prefetch=1,
            grid=(count,),
            in_specs=packed_specs(count, small_at)
            + SAVED_SPECS
            + [pl.BlockSpec((2, 2, DV, DK), lambda p, me: (p, 0, 0, 0))],
            out_specs=[pl.BlockSpec((CHUNK, width), lambda p, me: (0, 0))] * CHUNKS,
            scratch_shapes=[pltpu.VMEM((2, CHUNKS, 8, DK), f32)] + [pltpu.VMEM(square, f32)] * 3,
        ),
        out_shape=[jax.ShapeDtypeStruct((CHUNK, width), bf16)] * CHUNKS,
        compiler_params=pltpu.CompilerParams(vmem_limit_bytes=VMEM),
        cost_estimate=cost(count, 4_000_000_000),
        name="final_pass",
    )(me, *(list(packed) * 4), *small, *saved, states)


def turned(slots, way):
    count = lax.axis_size("head")
    return [slots[0]] + [
        lax.ppermute(slots[s], "head", [(i, (i + way * s) % count) for i in range(count)])
        for s in range(1, count)
    ]


def recursion(sends, place):
    segments = lax.axis_size("ctx")
    rows = segments // HEADS
    near = [[y * HEADS + r for r in range(HEADS)] for y in range(rows)]
    received = lax.all_to_all(
        sends, "ctx", split_axis=0, concat_axis=0, axis_index_groups=near, tiled=True
    )
    combined, before = combine_pass(place, received)
    others = [
        lax.ppermute(
            combined, "ctx", [(i, (i + s * HEADS) % segments) for i in range(segments)]
        )
        for s in range(1, rows)
    ]
    return lax.all_to_all(
        chain_pass(place, before, others),
        "ctx",
        split_axis=0,
        concat_axis=0,
        axis_index_groups=near,
        tiled=True,
    )


def on_device(query_rows, key_rows, value_rows, log_decay, beta_logit, out_grad):
    arrays = [query_rows, key_rows, value_rows, out_grad]
    gates = [log_decay.T, beta_logit.T]
    me = lax.axis_index("head").astype(jnp.int32).reshape(1)
    segment = lax.axis_index("ctx").astype(jnp.int32)
    rows = lax.axis_size("ctx") // HEADS
    place = jnp.stack([segment % 2, segment // HEADS, jnp.int32(rows)])
    received = []
    for b, e in GROUPS:
        slots = pack(me, arrays, gates if b == 0 else [], b, e)
        if received:
            slots, received[-1], place = lax.optimization_barrier((slots, received[-1], place))
        received.append(turned(slots, 1))
    small = received[0]
    small_at = small[0].shape[1] // 128 - 1
    saved, states, outs = [], [], []
    for (b, e), packed in zip(GROUPS, received):
        sends, *kept = local_pass(me, packed, small, small_at, b, e)
        saved.append(kept)
        found = recursion(sends.reshape(HEADS, PAYLOAD, DK), place)
        states.append(found.reshape(2 * (e - b), 2, DV, DK))
    for (b, e), packed, kept, state in zip(GROUPS, received, saved, states):
        outs.append(turned(final_pass(me, packed, small, small_at, kept, state, b, e), -1))
    return unpack(me, outs)


def solution(mesh):
    spec = P(("ctx", "head"), None)
    return jax.shard_map(
        on_device, mesh=mesh, in_specs=(spec,) * 6, out_specs=(spec,) * 5, check_vma=False
    )
```

```python
import functools

import jax
import jax.numpy as jnp
from jax import lax
from jax.experimental import pallas as pl
from jax.experimental.pallas import tpu as pltpu
from jax.sharding import PartitionSpec as P

DK = 128
DV = 128
CHUNK = 128
EPS = 1e-06
QUERY_SCALE = DK ** (-0.5)

KEY_HEADS = 4
HEADS = 8
CHUNKS = 4
GROUPS = ((0, 2), (2, 4))

PAYLOAD = DK + DV + 16
VMEM = 64 << 20

f32 = jnp.float32
bf16 = jnp.bfloat16

NN = (((1,), (0,)), ((), ()))
NT = (((1,), (1,)), ((), ()))
TN = (((0,), (0,)), ((), ()))

def dot(a, b, dims=NN):
    return lax.dot_general(a, b, dims, preferred_element_type=f32)

def low(x):
    return x.astype(bf16)

def split(x):
    high = x.astype(bf16)
    return high, (x - high.astype(f32)).astype(bf16)

def twice(a, axis):
    return jnp.concatenate([a, a], axis=axis)

def wide(x, axis):
    return jnp.concatenate(split(x), axis=axis)

def dot3(a, b, dims=NN):
    (ca,), (cb,) = dims[0]
    ah, al = split(a)
    bh, bl = split(b)
    return dot(
        jnp.concatenate([ah, al, ah], axis=ca), jnp.concatenate([bh, bh, bl], axis=cb), dims
    )

def grids(shape=(CHUNK, CHUNK)):
    return lax.broadcasted_iota(jnp.int32, shape, 0), lax.broadcasted_iota(jnp.int32, shape, 1)

def pickers(pair):
    row, col = grids((128, 4 * 128))
    spread = jnp.where(row == 2 * pair + (col // 128) % 2 + 8 * (col // 256), 1.0, 0.0)
    row, col = grids((32, 128))
    lines = jnp.where(col == 2 * pair + (row // 8) % 2 + 8 * (row // 16), 1.0, 0.0)
    return low(spread), low(lines)

def sigmoid(x):
    return 1.0 / (1.0 + jnp.exp(-x))

def unit_scale(x):
    return lax.rsqrt(jnp.sum(x * x, axis=1, keepdims=True) + EPS)

def chunk_terms(picks, qs, ks, smalls):
    row, col = grids()
    causal = row >= col
    eye = row == col
    spread, lines = picks
    lower = low(jnp.where(causal, 1.0, 0.0))
    upper = low(jnp.where(row <= col, 1.0, 0.0))
    key_keys = [dot(k, k, NT) for k in ks]
    query_keys = [dot(q, k, NT) for q, k in zip(qs, ks)]
    picked = [dot(small, spread) for small in smalls]
    picked_rows = [dot(lines, small, NT) for small in smalls]
    growth_cols = [dot(lower, low(x[:, :256])) for x in picked]
    growth_rows = [dot(low(x[:16]), upper) for x in picked_rows]
    terms = []
    for c in range(len(qs)):
        qf = qs[c].astype(f32)
        kf = ks[c].astype(f32)
        rk_col = unit_scale(kf)
        rk_row = lax.rsqrt(jnp.sum(jnp.where(eye, key_keys[c], 0.0), axis=0, keepdims=True) + EPS)
        rq_col = unit_scale(qf) * QUERY_SCALE
        heads = []
        for i in range(2):
            g_col = growth_cols[c][:, i * 128 : (i + 1) * 128]
            g_row = growth_rows[c][8 * i : 8 * i + 1]
            g_end = g_col[CHUNK - 1 : CHUNK, :]
            heads.append(
                dict(
                    decay=jnp.where(causal, jnp.exp(jnp.minimum(g_col - g_row, 0.0)), 0.0),
                    beta_col=sigmoid(picked[c][:, 256 + i * 128 : 384 + i * 128]),
                    beta_row=sigmoid(picked_rows[c][16 + 8 * i : 17 + 8 * i]),
                    growth_col=jnp.exp(g_col),
                    growth_row=jnp.exp(g_row),
                    to_end=jnp.exp(g_end - g_col),
                    keep=jnp.exp(g_end),
                )
            )
        terms.append(
            dict(
                key_key=key_keys[c] * (rk_col * rk_row),
                query_key=query_keys[c] * (rq_col * rk_row),
                rk_col=rk_col,
                rk_row=rk_row,
                rq_col=rq_col,
                qf=qf,
                kf=kf,
                heads=heads,
            )
        )
    return terms

def block_inverses(systems):
    size = 8
    count = CHUNK // size
    row, col = grids((size, CHUNK))
    own = [col // size == r for r in range(count)]
    packed = []
    for a in systems:
        rows = [jnp.where(own[r], a[r * size : (r + 1) * size], 0.0) for r in range(count)]
        while len(rows) > 1:
            rows = [x + y for x, y in zip(rows[::2], rows[1::2])]
        packed.append(rows[0])
    at, lane = grids((CHUNK, (size - 1) * CHUNK))
    spread = low(jnp.where(at == (lane % CHUNK) // size * size + lane // CHUNK, 1.0, 0.0))
    columns = dot(low(jnp.concatenate(packed, axis=0)), spread)
    found = [jnp.where(row == col % size, 1.0, 0.0) for _ in systems]
    for m in range(size - 1):
        found = [
            x - columns[n * size : (n + 1) * size, m * CHUNK : (m + 1) * CHUNK] * x[m : m + 1]
            for n, x in enumerate(found)
        ]
    return [
        jnp.concatenate([jnp.where(own[r], x, 0.0) for r in range(count)], axis=0) for x in found
    ]

def inverses(systems):
    row, col = grids()
    ident = jnp.where(row == col, 1.0, 0.0)
    found = block_inverses(systems)
    size = 8
    while size < CHUNK:
        merge = (row // (2 * size) == col // (2 * size)) & (row // size > col // size)
        parts = [low(jnp.where(merge, a, 0.0)) for a in systems]
        lows = [low(t) for t in found]
        inner = [dot(part, t) for part, t in zip(parts, lows)]
        found = [t - dot(tl, low(x)) for t, tl, x in zip(found, lows, inner)]
        size *= 2
    rests = [ident - t - dot3(a, t) for a, t in zip(systems, found)]
    return [t + dot(low(t), low(x)) for t, x in zip(found, rests)]

def slot_of(me, chunk):
    return lax.rem(me + CHUNKS - chunk, CHUNKS)

def in_order(me, slots):
    ordered = []
    for chunk in range(CHUNKS):
        found = slots[0]
        for slot in range(1, CHUNKS):
            found = jnp.where(lax.rem(me + CHUNKS - slot, CHUNKS) == chunk, slots[slot], found)
        ordered.append(found)
    return ordered

def slot_of(me, chunk):
    return lax.rem(me + CHUNKS - chunk, CHUNKS)

def inputs_of(me, refs):
    return [in_order(me, [r[...] for r in refs[n * CHUNKS : (n + 1) * CHUNKS]]) for n in range(5)]

def local_kernel(base, me_ref, *refs):
    ins, outs = refs[: 5 * CHUNKS], refs[5 * CHUNKS :]
    send_ref, w_ref, f_ref, t_ref, u_ref, d_ref, a_ref, l_ref = outs
    me = me_ref[0]
    pair = base + pl.program_id(0)
    row, col = grids()
    before = row > col
    chunks = CHUNKS
    qs, ks, vs, os, smalls = inputs_of(me, ins)
    terms = chunk_terms(pickers(pair), qs, ks, smalls)
    cases = [(c, i) for c in range(chunks) for i in range(2)]
    gates = [terms[c]["heads"][i] for c, i in cases]
    o_in = [os[c][:, i * DV : (i + 1) * DV] for c, i in cases]
    v_in = [vs[c][:, i * DV : (i + 1) * DV] for c, i in cases]
    systems = [
        jnp.where(before, h["beta_col"] * h["decay"] * terms[c]["key_key"], 0.0)
        for (c, i), h in zip(cases, gates)
    ]
    solved = inverses(systems)
    fresh = [
        dot(wide(h["decay"] * terms[c]["query_key"], 0), twice(o, 0), TN)
        for (c, i), h, o in zip(cases, gates, o_in)
    ]
    key_part = [
        dot(wide(t * (h["beta_row"] * h["growth_row"] * terms[c]["rk_row"]), 1), twice(ks[c], 0))
        for (c, i), h, t in zip(cases, gates, solved)
    ]
    value_part = [
        dot(wide(t * h["beta_row"], 1), twice(v, 0)) for h, t, v in zip(gates, solved, v_in)
    ]
    stepped = []
    for (c, i), h, x, y in zip(cases, gates, key_part, value_part):
        to_end = terms[c]["rk_col"] * h["to_end"]
        both = jnp.concatenate([-(to_end * x), to_end * y], axis=1)
        stepped.append(dot(wide(both, 0), twice(ks[c], 0), TN))
    devs = [x[:DK] for x in stepped]
    adds = [x[DK:] for x in stepped]
    backs = []
    for (c, i), h, u, w, o in zip(cases, gates, fresh, key_part, o_in):
        fh, fl = split(u)
        wh, wl = split(w)
        oh, ol = split(o.astype(f32) * (h["growth_col"] * terms[c]["rq_col"]))
        backs.append(
            dot(
                jnp.concatenate([oh, ol, -fh, -fl, -fh], axis=0),
                jnp.concatenate([qs[c], qs[c], wh, wh, wl], axis=0),
                TN,
            )
        )
    for n, (c, i) in enumerate(cases):
        slot = slot_of(me, c)
        w_ref[i, slot] = low(key_part[n])
        f_ref[i, slot] = value_part[n]
        t_ref[i, slot] = low(solved[n])
        u_ref[i, slot] = fresh[n]
        d_ref[i, slot] = low(devs[n])
        a_ref[i, slot] = adds[n]
        l_ref[i, slot] = backs[n]
    at = lambda c, i: 2 * c + i
    stacks = [jnp.concatenate([devs[i], adds[i]], axis=0) for i in range(2)]
    keeps = [gates[i]["keep"] for i in range(2)]
    grads = [backs[at(chunks - 1, i)] for i in range(2)]
    for step in range(1, chunks):
        back = chunks - 1 - step
        ahead = [dot3(stacks[i], devs[at(step, i)]) for i in range(2)]
        behind = [dot3(grads[i], devs[at(back, i)], NT) for i in range(2)]
        for i in range(2):
            n, m = at(step, i), at(back, i)
            keep = gates[n]["keep"]
            stacks[i] = (
                keep * stacks[i]
                + ahead[i]
                + jnp.concatenate([keeps[i] * devs[n], adds[n]], axis=0)
            )
            keeps[i] = keeps[i] * keep
            grads[i] = gates[m]["keep"] * grads[i] + behind[i] + backs[m]
    for i in range(2):
        high, rest = split(keeps[i])
        middle, last = split(keeps[i] - high.astype(f32))
        line = lax.broadcasted_iota(jnp.int32, (16, DK), 0)
        scale = jnp.where(line == 2, last.astype(f32), 0.0)
        scale = jnp.where(line == 1, middle.astype(f32), scale)
        scale = low(jnp.where(line == 0, high.astype(f32), scale))
        dev, add = stacks[i][:DK], stacks[i][DK:]
        for way, (step_map, addend) in enumerate(((dev, add), (dev.T, grads[i]))):
            send_ref[i, way, :DK] = low(step_map)
            send_ref[i, way, DK : DK + DV] = low(addend)
            send_ref[i, way, DK + DV :] = scale

def segment_parts(block):
    scale = jnp.sum(block[DK + DV :].astype(f32), axis=0, keepdims=True)
    return block[:DK], block[DK : DK + DV].astype(f32), scale

def combine_kernel(where_ref, x_ref, out_ref, before_ref):
    count = x_ref.shape[0]
    flip = where_ref[0]
    order = [jnp.where(flip == 1, count - 1 - step, step) for step in range(count)]
    parts = [segment_parts(x_ref[at]) for at in order]
    stacks = [jnp.concatenate([m.astype(f32), addend], axis=0) for m, addend, _ in parts]
    keeps = [scale for _, _, scale in parts]
    reach = 1
    while reach < count:
        joined = range(reach, count)
        if reach == 1:
            met = [dot(low(stacks[n - 1]), parts[n][0]) for n in joined]
        else:
            met = [dot3(stacks[n - reach], stacks[n][:DK]) for n in joined]
        met = [
            keeps[n] * stacks[n - reach]
            + x
            + jnp.concatenate([keeps[n - reach] * stacks[n][:DK], stacks[n][DK:]], axis=0)
            for n, x in zip(joined, met)
        ]
        stacks = stacks[:reach] + met
        keeps = keeps[:reach] + [keeps[n] * keeps[n - reach] for n in joined]
        reach *= 2
    stacks = [jnp.zeros_like(stacks[0])] + stacks
    keeps = [jnp.ones_like(keeps[0])] + keeps
    for step, at in enumerate(order):
        before_ref[at, : DK + DV] = stacks[step]
        before_ref[at, DK + DV :] = jnp.broadcast_to(keeps[step], (8, DK))
    out_ref[: DK + DV] = stacks[count]
    out_ref[DK + DV :] = jnp.broadcast_to(keeps[count], (8, DK))

def chain_kernel(where_ref, before_ref, one_ref, two_ref, three_ref, out_ref):
    flip = where_ref[0]
    place = where_ref[1]
    rows = where_ref[2]
    state = jnp.zeros((DV, DK), f32)
    for n, ahead, back in ((3, three_ref, one_ref), (2, two_ref, two_ref), (1, one_ref, three_ref)):
        block = jnp.where(flip == 1, back[...], ahead[...])
        there = jnp.where(flip == 1, place + n < rows, n <= place)
        later = block[DK + DV : DK + DV + 1] * state + block[DK : DK + DV]
        if n < 3:
            later = later + dot3(state, block[:DK])
        state = jnp.where(there, later, state)
    for step in range(before_ref.shape[0]):
        keep = before_ref[step, DK + DV : DK + DV + 1]
        met = dot3(state, before_ref[step, :DK])
        out_ref[step] = low(keep * state + met + before_ref[step, DK : DK + DV])

def final_kernel(base, me_ref, *refs):
    ins, refs = refs[: 5 * CHUNKS], refs[5 * CHUNKS :]
    w_ref, f_ref, t_ref, u_ref, d_ref, a_ref, l_ref, h_ref = refs[:8]
    out_refs = refs[8 : 8 + CHUNKS]
    keep_ref, state_ref, after_ref, grad_ref = refs[8 + CHUNKS :]
    me = me_ref[0]
    here = pl.program_id(0)
    pair = base + here
    row, col = grids()
    before = row > col
    suffix = low(jnp.where(row <= col, 1.0, 0.0))
    chunks = CHUNKS
    qs, ks, vs, os, smalls = ([r[...] for r in ins[n * chunks : (n + 1) * chunks]] for n in range(5))
    terms = chunk_terms(pickers(pair), qs, ks, smalls)
    cases = [(c, i) for c in range(chunks) for i in range(2)]
    gates = [terms[c]["heads"][i] for c, i in cases]
    o_in = [os[c][:, i * DV : (i + 1) * DV] for c, i in cases]

    for n, (c, i) in enumerate(cases):
        keep_ref[i, c] = jnp.broadcast_to(gates[n]["keep"], (8, DK))
    states = [h_ref[i, 0].astype(f32) for i in range(2)]
    grads = [h_ref[i, 1].astype(f32) for i in range(2)]
    for step in range(chunks):
        n, m = slot_of(me, step), slot_of(me, chunks - 1 - step)
        for i in range(2):
            state_ref[i, n] = states[i]
            grad_ref[i, m] = grads[i]
        ahead = [dot(wide(states[i], 1), twice(d_ref[i, n], 0)) for i in range(2)]
        if step < chunks - 1:
            behind = [dot(wide(grads[i], 1), twice(d_ref[i, m], 1), NT) for i in range(2)]
        for i in range(2):
            states[i] = keep_ref[i, n][:1] * states[i] + ahead[i] + a_ref[i, n]
            after_ref[i, n] = states[i]
            if step < chunks - 1:
                grads[i] = keep_ref[i, m][:1] * grads[i] + behind[i] + l_ref[i, m]
    state_of = [state_ref[i, c] for c, i in cases]
    after_of = [after_ref[i, c] for c, i in cases]
    grad_of = [grad_ref[i, c] for c, i in cases]

    fresh = [
        f_ref[i, c] - dot(twice(w_ref[i, c], 1), wide(state, 1), NT)
        for (c, i), state in zip(cases, state_of)
    ]
    fresh_grad = [
        u_ref[i, c]
        + (terms[c]["rk_col"] * h["to_end"]) * dot(twice(ks[c], 1), wide(grad, 1), NT)
        for (c, i), h, grad in zip(cases, gates, grad_of)
    ]
    solved = [
        dot(twice(t_ref[i, c], 0), wide(x, 0), TN) for (c, i), x in zip(cases, fresh_grad)
    ]
    value_grad = [h["beta_col"] * x for h, x in zip(gates, solved)]
    quarter = (out_refs[0].shape[1] - 128) // 4
    for (c, i), x in zip(cases, value_grad):
        start = 2 * quarter + here * (2 * DV) + i * DV
        out_refs[c][:, pl.ds(pl.multiple_of(start, DV), DV)] = low(x)
    sides = [jnp.concatenate([low(x), o], axis=0) for x, o in zip(value_grad, o_in)]
    fresh_low = [low(x) for x in fresh]
    outer = [dot(x, low(state)) for x, state in zip(sides, state_of)]
    ended = [
        h["to_end"] * dot(x, low(grad)) for h, x, grad in zip(gates, fresh_low, grad_of)
    ]
    inner = [dot(x, y, NT) for x, y in zip(sides, fresh_low)]
    key_read = [-h["growth_col"] * x[:CHUNK] for h, x in zip(gates, outer)]
    query_read = [h["growth_col"] * x[CHUNK:] for h, x in zip(gates, outer)]
    erase = [jnp.where(before, h["decay"] * x[:CHUNK], 0.0) for h, x in zip(gates, inner)]
    read = [h["decay"] * x[CHUNK:] for h, x in zip(gates, inner)]
    units = [(t["qf"] * t["rq_col"], t["kf"] * t["rk_col"]) for t in terms]
    sums = []
    for n, (c, i) in enumerate(cases):
        query_unit, key_unit = units[c]
        spread = read[n] * terms[c]["query_key"] - erase[n] * terms[c]["key_key"]
        lone = query_unit * query_read[n] + key_unit * (key_read[n] - ended[n])
        sums.append(dot(twice(suffix, 1), wide(jnp.concatenate([spread, lone], axis=1), 0)))
    query_inner, key_inner = [], []
    for c in range(chunks):
        term = terms[c]
        read_sum = read[2 * c] + read[2 * c + 1]
        erase_sum = erase[2 * c] + erase[2 * c + 1]
        query_inner.append(dot(wide(read_sum * term["rk_row"], 1), twice(ks[c], 0)))
        key_inner.append(
            dot(wide(erase_sum * -term["rk_row"], 1), twice(ks[c], 0))
            + dot(
                jnp.concatenate(
                    split(read_sum * term["rq_col"]) + split(erase_sum * -term["rk_col"]), axis=0
                ),
                jnp.concatenate([qs[c], qs[c], ks[c], ks[c]], axis=0),
                TN,
            )
        )
    small_out = []
    for c in range(chunks):
        parts, places = [], []
        wholes = 0.0
        for i in range(2):
            n = 2 * c + i
            at = 2 * pair + i
            for place, part in (
                (at, jnp.where(before, sums[n][:, :CHUNK], 0.0) + sums[n][:, CHUNK:]),
                (at + 8, (1.0 - gates[n]["beta_col"]) * solved[n] * fresh[n]),
            ):
                parts += split(part)
                places += [low(jnp.where(col == place, 1.0, 0.0))] * 2
            product = jnp.sum(grad_of[n] * after_of[n], axis=0, keepdims=True)
            whole = jnp.sum(product, axis=1, keepdims=True)
            wholes = wholes + jnp.where(col[:1] == at, whole, 0.0)
        small_out.append(
            dot(jnp.concatenate(parts, axis=1), jnp.concatenate(places, axis=0)) + wholes
        )
    for c in range(chunks):
        term = terms[c]
        query_unit, key_unit = units[c]
        query_grad = query_inner[c] + query_read[2 * c] + query_read[2 * c + 1]
        key_grad = (
            key_inner[c]
            + (key_read[2 * c] + ended[2 * c])
            + (key_read[2 * c + 1] + ended[2 * c + 1])
        )
        query_back = term["rq_col"] * (
            query_grad
            - query_unit * (DK * jnp.sum(query_unit * query_grad, axis=1, keepdims=True))
        )
        key_back = term["rk_col"] * (
            key_grad - key_unit * jnp.sum(key_unit * key_grad, axis=1, keepdims=True)
        )
        out_refs[c][:, pl.ds(pl.multiple_of(here * DK, DK), DK)] = low(query_back)
        out_refs[c][:, pl.ds(pl.multiple_of(quarter + here * DK, DK), DK)] = low(key_back)
        place = slice(4 * quarter, 4 * quarter + 128)
        mine = (col // 2 == pair) | (col // 2 == pair + 4)
        held = out_refs[c][:, place]
        kept = jnp.where(here == 0, jnp.zeros_like(held), held)
        out_refs[c][:, place] = jnp.where(mine, low(small_out[c]), kept)

def pack_kernel(me_ref, *refs):
    outs = refs[-CHUNKS:]
    for slot, out_ref in enumerate(outs):
        at = 0
        for ref in refs[4 * slot : 4 * slot + 4]:
            width = ref.shape[1]
            out_ref[:, at : at + width] = ref[...]
            at += width
    if len(refs) > 5 * CHUNKS:
        d_ref, b_ref = refs[4 * CHUNKS : 4 * CHUNKS + 2]
        for slot, out_ref in enumerate(outs):
            dest = lax.rem(me_ref[0] + slot, CHUNKS)
            row, col = grids((d_ref.shape[0], 128))
            decays = (col < HEADS) & (row == HEADS * dest + col)
            betas = (col >= HEADS) & (col < 2 * HEADS) & (row == HEADS * dest + col - HEADS)
            picks = [low(jnp.where(here, 1.0, 0.0)) for here in (decays, betas)]
            out_ref[:, at : at + 128] = low(
                dot(d_ref[...], picks[0], TN) + dot(b_ref[...], picks[1], TN)
            )

def pack(me, arrays, gates, begin, end):
    count = end - begin
    per = KEY_HEADS // count
    first = begin // count
    widths = [count * size for size in (DK, DK, 2 * DV, 2 * DV)]
    total = sum(widths) + (128 if gates else 0)
    specs = []
    for slot in range(CHUNKS):
        for width in widths:
            specs.append(
                pl.BlockSpec(
                    (CHUNK, width),
                    lambda g, me, slot=slot: (0, per * lax.rem(me[0] + slot, CHUNKS) + first),
                )
            )
    return pl.pallas_call(
        pack_kernel,
        grid_spec=pltpu.PrefetchScalarGridSpec(
            num_scalar_prefetch=1,
            grid=(1,),
            in_specs=specs + [pl.BlockSpec(gate.shape, lambda g, me: (0, 0)) for gate in gates],
            out_specs=[pl.BlockSpec((CHUNK, total), lambda g, me: (0, 0))] * CHUNKS,
        ),
        out_shape=[jax.ShapeDtypeStruct((CHUNK, total), bf16)] * CHUNKS,
        compiler_params=pltpu.CompilerParams(vmem_limit_bytes=VMEM),
        name="pack",
    )(me, *(list(arrays) * CHUNKS), *gates)

def unpack_kernel(me_ref, *refs):
    arrived = refs[: len(GROUPS) * CHUNKS]
    q_ref, k_ref, v_ref, d_ref, b_ref = refs[len(GROUPS) * CHUNKS :]
    d_sum, b_sum = 0.0, 0.0
    row, col = grids((d_ref.shape[0], 128))
    for g, (begin, end) in enumerate(GROUPS):
        for slot in range(CHUNKS):
            ref = arrived[g * CHUNKS + slot]
            source = lax.rem(me_ref[0] + slot, CHUNKS)
            at = 0
            for out, size in ((q_ref, DK), (k_ref, DK), (v_ref, 2 * DV)):
                width = (end - begin) * size
                start = pl.multiple_of((source * KEY_HEADS + begin) * size, 128)
                out[:, pl.ds(start, width)] = ref[:, at : at + width]
                at += width
            small = ref[:, at : at + 128]
            decays = (col < HEADS) & (row == HEADS * source + col)
            betas = (col >= HEADS) & (col < 2 * HEADS) & (row == HEADS * source + col - HEADS)
            d_sum = d_sum + dot(low(jnp.where(decays, 1.0, 0.0)), small, NT)
            b_sum = b_sum + dot(low(jnp.where(betas, 1.0, 0.0)), small, NT)
    d_ref[...] = low(d_sum)
    b_ref[...] = low(b_sum)

def whole(shape):
    return pl.BlockSpec(shape, lambda g, me: (0,) * len(shape))

def unpack(me, groups):
    arrived = [x for group in groups for x in group]
    shapes = [(CHUNK, CHUNKS * size) for size in (KEY_HEADS * DK, KEY_HEADS * DK, HEADS * DV)]
    shapes += [(CHUNKS * HEADS, CHUNK)] * 2
    q, k, v, d, b = pl.pallas_call(
        unpack_kernel,
        grid_spec=pltpu.PrefetchScalarGridSpec(
            num_scalar_prefetch=1,
            grid=(1,),
            in_specs=[whole(x.shape) for x in arrived],
            out_specs=[whole(shape) for shape in shapes],
        ),
        out_shape=[jax.ShapeDtypeStruct(shape, bf16) for shape in shapes],
        compiler_params=pltpu.CompilerParams(vmem_limit_bytes=VMEM),
        name="unpack",
    )(me, *arrived)
    return q, k, v, d.T, b.T

def packed_specs(count, small_at, off=0):
    return (
        [pl.BlockSpec((CHUNK, DK), lambda p, me: (0, off + p))] * CHUNKS
        + [pl.BlockSpec((CHUNK, DK), lambda p, me: (0, count + off + p))] * CHUNKS
        + [pl.BlockSpec((CHUNK, 2 * DV), lambda p, me: (0, count + off + p))] * CHUNKS
        + [pl.BlockSpec((CHUNK, 2 * DV), lambda p, me: (0, 2 * count + off + p))] * CHUNKS
        + [pl.BlockSpec((CHUNK, 128), lambda p, me: (0, small_at))] * CHUNKS
    )

SAVED = (bf16, f32, bf16, f32, bf16, f32, f32)

def saved_specs(off=0):
    square = (2, CHUNKS, CHUNK, CHUNK)
    return [pl.BlockSpec(square, lambda p, me: (off + p, 0, 0, 0)) for _ in SAVED]

def cost(count, flops):
    return pl.CostEstimate(flops=count * flops, bytes_accessed=count * 5_000_000, transcendentals=0)

def local_pass(me, packed, small, small_at, begin, end):
    count = end - begin
    return pl.pallas_call(
        functools.partial(local_kernel, begin),
        grid_spec=pltpu.PrefetchScalarGridSpec(
            num_scalar_prefetch=1,
            grid=(count,),
            in_specs=packed_specs(count, small_at),
            out_specs=[pl.BlockSpec((2, 2, PAYLOAD, DK), lambda p, me: (p, 0, 0, 0))] + saved_specs(),
        ),
        out_shape=[jax.ShapeDtypeStruct((2 * count, 2, PAYLOAD, DK), bf16)]
        + [jax.ShapeDtypeStruct((2 * count, CHUNKS, CHUNK, CHUNK), kind) for kind in SAVED],
        compiler_params=pltpu.CompilerParams(vmem_limit_bytes=VMEM),
        cost_estimate=cost(count, 4_000_000_000),
        name="local_pass",
    )(me, *(list(packed) * 4), *small)

def combine_pass(place, received):
    shape = (DK + DV + 8, DK)
    each = (received.shape[0],) + shape
    return pl.pallas_call(
        combine_kernel,
        grid_spec=pltpu.PrefetchScalarGridSpec(
            num_scalar_prefetch=1,
            grid=(1,),
            in_specs=[whole(received.shape)],
            out_specs=[whole(shape), whole(each)],
        ),
        out_shape=[jax.ShapeDtypeStruct(shape, f32), jax.ShapeDtypeStruct(each, f32)],
        compiler_params=pltpu.CompilerParams(vmem_limit_bytes=VMEM),
        cost_estimate=cost(1, 1_500_000_000),
        name="combine_pass",
    )(place, received)

def chain_pass(place, before, others):
    shape = (before.shape[0], DV, DK)
    return pl.pallas_call(
        chain_kernel,
        grid_spec=pltpu.PrefetchScalarGridSpec(
            num_scalar_prefetch=1,
            grid=(1,),
            in_specs=[whole(before.shape)] + [whole(x.shape) for x in others],
            out_specs=whole(shape),
        ),
        out_shape=jax.ShapeDtypeStruct(shape, bf16),
        compiler_params=pltpu.CompilerParams(vmem_limit_bytes=VMEM),
        cost_estimate=cost(1, 1_500_000_000),
        name="chain_pass",
    )(place, before, *others)

def final_pass(me, packed, small, small_at, saved, states, group, begin, end):
    count = end - begin
    held, off = group[1] - group[0], begin - group[0]
    width = count * 2 * (DK + DV) + 128
    square = (2, CHUNKS, DV, DK)
    return pl.pallas_call(
        functools.partial(final_kernel, begin),
        grid_spec=pltpu.PrefetchScalarGridSpec(
            num_scalar_prefetch=1,
            grid=(count,),
            in_specs=packed_specs(held, small_at, off)
            + saved_specs(off)
            + [pl.BlockSpec((2, 2, DV, DK), lambda p, me: (off + p, 0, 0, 0))],
            out_specs=[pl.BlockSpec((CHUNK, width), lambda p, me: (0, 0))] * CHUNKS,
            scratch_shapes=[pltpu.VMEM((2, CHUNKS, 8, DK), f32)] + [pltpu.VMEM(square, f32)] * 3,
        ),
        out_shape=[jax.ShapeDtypeStruct((CHUNK, width), bf16)] * CHUNKS,
        compiler_params=pltpu.CompilerParams(vmem_limit_bytes=VMEM),
        cost_estimate=cost(count, 4_000_000_000),
        name="final_pass",
    )(me, *(list(packed) * 4), *small, *saved, states)

def turned(slots, way):
    count = lax.axis_size("head")
    return [slots[0]] + [
        lax.ppermute(slots[s], "head", [(i, (i + way * s) % count) for i in range(count)])
        for s in range(1, count)
    ]

def recursion(sends, place):
    segments = lax.axis_size("ctx")
    rows = segments // HEADS
    near = [[y * HEADS + r for r in range(HEADS)] for y in range(rows)]
    received = lax.all_to_all(
        sends, "ctx", split_axis=0, concat_axis=0, axis_index_groups=near, tiled=True
    )
    combined, before = combine_pass(place, received)
    others = [
        lax.ppermute(
            combined, "ctx", [(i, (i + s * HEADS) % segments) for i in range(segments)]
        )
        for s in range(1, rows)
    ]
    return lax.all_to_all(
        chain_pass(place, before, others),
        "ctx",
        split_axis=0,
        concat_axis=0,
        axis_index_groups=near,
        tiled=True,
    )

def on_device(query_rows, key_rows, value_rows, log_decay, beta_logit, out_grad):
    arrays = [query_rows, key_rows, value_rows, out_grad]
    gates = [log_decay.T, beta_logit.T]
    me = lax.axis_index("head").astype(jnp.int32).reshape(1)
    segment = lax.axis_index("ctx").astype(jnp.int32)
    rows = lax.axis_size("ctx") // HEADS
    place = jnp.stack([segment % 2, segment // HEADS, jnp.int32(rows)])
    received = []
    for b, e in GROUPS:
        slots = pack(me, arrays, gates if b == 0 else [], b, e)
        if received:
            slots, received[-1], place = lax.optimization_barrier((slots, received[-1], place))
        received.append(turned(slots, 1))
    small = received[0]
    small_at = small[0].shape[1] // 128 - 1
    saved, states, outs = [], [], []
    for (b, e), packed in zip(GROUPS, received):
        sends, *kept = local_pass(me, packed, small, small_at, b, e)
        saved.append(kept)
        found = recursion(sends.reshape(HEADS, PAYLOAD, DK), place)
        states.append(found.reshape(2 * (e - b), 2, DV, DK))
    for b, e in GROUPS:
        n = [g for g, (first, last) in enumerate(GROUPS) if first <= b < last][0]
        grads = final_pass(
            me, received[n], small, small_at, saved[n], states[n], GROUPS[n], b, e
        )
        outs.append(turned(grads, -1))
    return unpack(me, outs)

def solution(mesh):
    spec = P(("ctx", "head"), None)
    return jax.shard_map(
        on_device, mesh=mesh, in_specs=(spec,) * 6, out_specs=(spec,) * 5, check_vma=False
    )
```

```python
import functools

import jax
import jax.numpy as jnp
from jax import lax
from jax.experimental import pallas as pl
from jax.experimental.pallas import tpu as pltpu
from jax.sharding import PartitionSpec as P

DK = 128
DV = 128
CHUNK = 128
EPS = 1e-06
QUERY_SCALE = DK ** (-0.5)

KEY_HEADS = 4
HEADS = 8
CHUNKS = 4
GROUPS = ((0, 2), (2, 4))

PAYLOAD = DK + DV + 16
VMEM = 64 << 20

f32 = jnp.float32
bf16 = jnp.bfloat16

NN = (((1,), (0,)), ((), ()))
NT = (((1,), (1,)), ((), ()))
TN = (((0,), (0,)), ((), ()))

def dot(a, b, dims=NN):
    return lax.dot_general(a, b, dims, preferred_element_type=f32)

def low(x):
    return x.astype(bf16)

def split(x):
    high = x.astype(bf16)
    return high, (x - high.astype(f32)).astype(bf16)

def twice(a, axis):
    return jnp.concatenate([a, a], axis=axis)

def wide(x, axis):
    return jnp.concatenate(split(x), axis=axis)

def dot3(a, b, dims=NN):
    (ca,), (cb,) = dims[0]
    ah, al = split(a)
    bh, bl = split(b)
    return dot(
        jnp.concatenate([ah, al, ah], axis=ca), jnp.concatenate([bh, bh, bl], axis=cb), dims
    )

def grids(shape=(CHUNK, CHUNK)):
    return lax.broadcasted_iota(jnp.int32, shape, 0), lax.broadcasted_iota(jnp.int32, shape, 1)

def pickers(pair):
    row, col = grids((128, 4 * 128))
    spread = jnp.where(row == 2 * pair + (col // 128) % 2 + 8 * (col // 256), 1.0, 0.0)
    row, col = grids((32, 128))
    lines = jnp.where(col == 2 * pair + (row // 8) % 2 + 8 * (row // 16), 1.0, 0.0)
    return low(spread), low(lines)

def sigmoid(x):
    return 1.0 / (1.0 + jnp.exp(-x))

def unit_scale(x):
    return lax.rsqrt(jnp.sum(x * x, axis=1, keepdims=True) + EPS)

def chunk_terms(picks, qs, ks, smalls):
    row, col = grids()
    causal = row >= col
    eye = row == col
    spread, lines = picks
    lower = low(jnp.where(causal, 1.0, 0.0))
    upper = low(jnp.where(row <= col, 1.0, 0.0))
    key_keys = [dot(k, k, NT) for k in ks]
    query_keys = [dot(q, k, NT) for q, k in zip(qs, ks)]
    picked = [dot(small, spread) for small in smalls]
    picked_rows = [dot(lines, small, NT) for small in smalls]
    growth_cols = [dot(lower, low(x[:, :256])) for x in picked]
    growth_rows = [dot(low(x[:16]), upper) for x in picked_rows]
    terms = []
    for c in range(len(qs)):
        qf = qs[c].astype(f32)
        kf = ks[c].astype(f32)
        rk_col = unit_scale(kf)
        rk_row = lax.rsqrt(jnp.sum(jnp.where(eye, key_keys[c], 0.0), axis=0, keepdims=True) + EPS)
        rq_col = unit_scale(qf) * QUERY_SCALE
        heads = []
        for i in range(2):
            g_col = growth_cols[c][:, i * 128 : (i + 1) * 128]
            g_row = growth_rows[c][8 * i : 8 * i + 1]
            g_end = g_col[CHUNK - 1 : CHUNK, :]
            heads.append(
                dict(
                    decay=jnp.where(causal, jnp.exp(jnp.minimum(g_col - g_row, 0.0)), 0.0),
                    beta_col=sigmoid(picked[c][:, 256 + i * 128 : 384 + i * 128]),
                    beta_row=sigmoid(picked_rows[c][16 + 8 * i : 17 + 8 * i]),
                    growth_col=jnp.exp(g_col),
                    growth_row=jnp.exp(g_row),
                    to_end=jnp.exp(g_end - g_col),
                    keep=jnp.exp(g_end),
                )
            )
        terms.append(
            dict(
                key_key=key_keys[c] * (rk_col * rk_row),
                query_key=query_keys[c] * (rq_col * rk_row),
                rk_col=rk_col,
                rk_row=rk_row,
                rq_col=rq_col,
                qf=qf,
                kf=kf,
                heads=heads,
            )
        )
    return terms

def block_inverses(systems):
    size = 8
    count = CHUNK // size
    row, col = grids((size, CHUNK))
    own = [col // size == r for r in range(count)]
    packed = []
    for a in systems:
        rows = [jnp.where(own[r], a[r * size : (r + 1) * size], 0.0) for r in range(count)]
        while len(rows) > 1:
            rows = [x + y for x, y in zip(rows[::2], rows[1::2])]
        packed.append(rows[0])
    at, lane = grids((CHUNK, (size - 1) * CHUNK))
    spread = low(jnp.where(at == (lane % CHUNK) // size * size + lane // CHUNK, 1.0, 0.0))
    columns = dot(low(jnp.concatenate(packed, axis=0)), spread)
    found = [jnp.where(row == col % size, 1.0, 0.0) for _ in systems]
    for m in range(size - 1):
        found = [
            x - columns[n * size : (n + 1) * size, m * CHUNK : (m + 1) * CHUNK] * x[m : m + 1]
            for n, x in enumerate(found)
        ]
    return [
        jnp.concatenate([jnp.where(own[r], x, 0.0) for r in range(count)], axis=0) for x in found
    ]

def inverses(systems):
    row, col = grids()
    ident = jnp.where(row == col, 1.0, 0.0)
    found = block_inverses(systems)
    size = 8
    while size < CHUNK:
        merge = (row // (2 * size) == col // (2 * size)) & (row // size > col // size)
        parts = [low(jnp.where(merge, a, 0.0)) for a in systems]
        lows = [low(t) for t in found]
        inner = [dot(part, t) for part, t in zip(parts, lows)]
        found = [t - dot(tl, low(x)) for t, tl, x in zip(found, lows, inner)]
        size *= 2
    rests = [ident - t - dot3(a, t) for a, t in zip(systems, found)]
    return [t + dot(low(t), low(x)) for t, x in zip(found, rests)]

def slot_of(me, chunk):
    return lax.rem(me + CHUNKS - chunk, CHUNKS)

def in_order(me, slots):
    ordered = []
    for chunk in range(CHUNKS):
        found = slots[0]
        for slot in range(1, CHUNKS):
            found = jnp.where(lax.rem(me + CHUNKS - slot, CHUNKS) == chunk, slots[slot], found)
        ordered.append(found)
    return ordered

def slot_of(me, chunk):
    return lax.rem(me + CHUNKS - chunk, CHUNKS)

def inputs_of(me, refs):
    return [in_order(me, [r[...] for r in refs[n * CHUNKS : (n + 1) * CHUNKS]]) for n in range(5)]

def local_kernel(base, me_ref, *refs):
    ins, outs = refs[: 5 * CHUNKS], refs[5 * CHUNKS :]
    send_ref, w_ref, f_ref, t_ref, u_ref, d_ref, a_ref, l_ref = outs
    me = me_ref[0]
    pair = base + pl.program_id(0)
    row, col = grids()
    before = row > col
    chunks = CHUNKS
    qs, ks, vs, os, smalls = inputs_of(me, ins)
    terms = chunk_terms(pickers(pair), qs, ks, smalls)
    cases = [(c, i) for c in range(chunks) for i in range(2)]
    gates = [terms[c]["heads"][i] for c, i in cases]
    o_in = [os[c][:, i * DV : (i + 1) * DV] for c, i in cases]
    v_in = [vs[c][:, i * DV : (i + 1) * DV] for c, i in cases]
    systems = [
        jnp.where(before, h["beta_col"] * h["decay"] * terms[c]["key_key"], 0.0)
        for (c, i), h in zip(cases, gates)
    ]
    solved = inverses(systems)
    fresh = [
        dot(wide(h["decay"] * terms[c]["query_key"], 0), twice(o, 0), TN)
        for (c, i), h, o in zip(cases, gates, o_in)
    ]
    key_part = [
        dot(wide(t * (h["beta_row"] * h["growth_row"] * terms[c]["rk_row"]), 1), twice(ks[c], 0))
        for (c, i), h, t in zip(cases, gates, solved)
    ]
    value_part = [
        dot(wide(t * h["beta_row"], 1), twice(v, 0)) for h, t, v in zip(gates, solved, v_in)
    ]
    stepped = []
    for (c, i), h, x, y in zip(cases, gates, key_part, value_part):
        to_end = terms[c]["rk_col"] * h["to_end"]
        both = jnp.concatenate([-(to_end * x), to_end * y], axis=1)
        stepped.append(dot(wide(both, 0), twice(ks[c], 0), TN))
    devs = [x[:DK] for x in stepped]
    adds = [x[DK:] for x in stepped]
    backs = []
    for (c, i), h, u, w, o in zip(cases, gates, fresh, key_part, o_in):
        fh, fl = split(u)
        wh, wl = split(w)
        oh, ol = split(o.astype(f32) * (h["growth_col"] * terms[c]["rq_col"]))
        backs.append(
            dot(
                jnp.concatenate([oh, ol, -fh, -fl, -fh], axis=0),
                jnp.concatenate([qs[c], qs[c], wh, wh, wl], axis=0),
                TN,
            )
        )
    for n, (c, i) in enumerate(cases):
        slot = slot_of(me, c)
        w_ref[i, slot] = low(key_part[n])
        f_ref[i, slot] = value_part[n]
        t_ref[i, slot] = solved[n]
        u_ref[i, slot] = fresh[n]
        d_ref[i, slot] = low(devs[n])
        a_ref[i, slot] = adds[n]
        l_ref[i, slot] = backs[n]
    at = lambda c, i: 2 * c + i
    stacks = [jnp.concatenate([devs[i], adds[i]], axis=0) for i in range(2)]
    keeps = [gates[i]["keep"] for i in range(2)]
    grads = [backs[at(chunks - 1, i)] for i in range(2)]
    for step in range(1, chunks):
        back = chunks - 1 - step
        ahead = [dot3(stacks[i], devs[at(step, i)]) for i in range(2)]
        behind = [dot3(grads[i], devs[at(back, i)], NT) for i in range(2)]
        for i in range(2):
            n, m = at(step, i), at(back, i)
            keep = gates[n]["keep"]
            stacks[i] = (
                keep * stacks[i]
                + ahead[i]
                + jnp.concatenate([keeps[i] * devs[n], adds[n]], axis=0)
            )
            keeps[i] = keeps[i] * keep
            grads[i] = gates[m]["keep"] * grads[i] + behind[i] + backs[m]
    for i in range(2):
        high, rest = split(keeps[i])
        middle, last = split(keeps[i] - high.astype(f32))
        line = lax.broadcasted_iota(jnp.int32, (16, DK), 0)
        scale = jnp.where(line == 2, last.astype(f32), 0.0)
        scale = jnp.where(line == 1, middle.astype(f32), scale)
        scale = low(jnp.where(line == 0, high.astype(f32), scale))
        dev, add = stacks[i][:DK], stacks[i][DK:]
        for way, (step_map, addend) in enumerate(((dev, add), (dev.T, grads[i]))):
            send_ref[i, way, :DK] = low(step_map)
            send_ref[i, way, DK : DK + DV] = low(addend)
            send_ref[i, way, DK + DV :] = scale

def segment_parts(block):
    scale = jnp.sum(block[DK + DV :].astype(f32), axis=0, keepdims=True)
    return block[:DK], block[DK : DK + DV].astype(f32), scale

def combine_kernel(where_ref, x_ref, out_ref, before_ref):
    count = x_ref.shape[0]
    flip = where_ref[0]
    order = [jnp.where(flip == 1, count - 1 - step, step) for step in range(count)]
    parts = [segment_parts(x_ref[at]) for at in order]
    stacks = [jnp.concatenate([m.astype(f32), addend], axis=0) for m, addend, _ in parts]
    keeps = [scale for _, _, scale in parts]
    reach = 1
    while reach < count:
        joined = range(reach, count)
        if reach == 1:
            met = [dot(low(stacks[n - 1]), parts[n][0]) for n in joined]
        else:
            met = [dot3(stacks[n - reach], stacks[n][:DK]) for n in joined]
        met = [
            keeps[n] * stacks[n - reach]
            + x
            + jnp.concatenate([keeps[n - reach] * stacks[n][:DK], stacks[n][DK:]], axis=0)
            for n, x in zip(joined, met)
        ]
        stacks = stacks[:reach] + met
        keeps = keeps[:reach] + [keeps[n] * keeps[n - reach] for n in joined]
        reach *= 2
    stacks = [jnp.zeros_like(stacks[0])] + stacks
    keeps = [jnp.ones_like(keeps[0])] + keeps
    for step, at in enumerate(order):
        before_ref[at, : DK + DV] = stacks[step]
        before_ref[at, DK + DV :] = jnp.broadcast_to(keeps[step], (8, DK))
    out_ref[: DK + DV] = stacks[count]
    out_ref[DK + DV :] = jnp.broadcast_to(keeps[count], (8, DK))

def chain_kernel(where_ref, before_ref, one_ref, two_ref, three_ref, out_ref):
    flip = where_ref[0]
    place = where_ref[1]
    rows = where_ref[2]
    state = jnp.zeros((DV, DK), f32)
    for n, ahead, back in ((3, three_ref, one_ref), (2, two_ref, two_ref), (1, one_ref, three_ref)):
        block = jnp.where(flip == 1, back[...], ahead[...])
        there = jnp.where(flip == 1, place + n < rows, n <= place)
        later = block[DK + DV : DK + DV + 1] * state + block[DK : DK + DV]
        if n < 3:
            later = later + dot3(state, block[:DK])
        state = jnp.where(there, later, state)
    for step in range(before_ref.shape[0]):
        keep = before_ref[step, DK + DV : DK + DV + 1]
        met = dot3(state, before_ref[step, :DK])
        out_ref[step] = low(keep * state + met + before_ref[step, DK : DK + DV])

def final_kernel(base, me_ref, *refs):
    ins, refs = refs[: 5 * CHUNKS], refs[5 * CHUNKS :]
    w_ref, f_ref, t_ref, u_ref, d_ref, a_ref, l_ref, h_ref = refs[:8]
    out_refs = refs[8 : 8 + CHUNKS]
    keep_ref, state_ref, after_ref, grad_ref = refs[8 + CHUNKS :]
    me = me_ref[0]
    here = pl.program_id(0)
    pair = base + here
    row, col = grids()
    before = row > col
    suffix = low(jnp.where(row <= col, 1.0, 0.0))
    chunks = CHUNKS
    qs, ks, vs, os, smalls = ([r[...] for r in ins[n * chunks : (n + 1) * chunks]] for n in range(5))
    terms = chunk_terms(pickers(pair), qs, ks, smalls)
    cases = [(c, i) for c in range(chunks) for i in range(2)]
    gates = [terms[c]["heads"][i] for c, i in cases]
    o_in = [os[c][:, i * DV : (i + 1) * DV] for c, i in cases]

    for n, (c, i) in enumerate(cases):
        keep_ref[i, c] = jnp.broadcast_to(gates[n]["keep"], (8, DK))
    states = [h_ref[i, 0].astype(f32) for i in range(2)]
    grads = [h_ref[i, 1].astype(f32) for i in range(2)]
    for step in range(chunks):
        n, m = slot_of(me, step), slot_of(me, chunks - 1 - step)
        for i in range(2):
            state_ref[i, n] = states[i]
            grad_ref[i, m] = grads[i]
        ahead = [dot(wide(states[i], 1), twice(d_ref[i, n], 0)) for i in range(2)]
        if step < chunks - 1:
            behind = [dot(wide(grads[i], 1), twice(d_ref[i, m], 1), NT) for i in range(2)]
        for i in range(2):
            states[i] = keep_ref[i, n][:1] * states[i] + ahead[i] + a_ref[i, n]
            after_ref[i, n] = states[i]
            if step < chunks - 1:
                grads[i] = keep_ref[i, m][:1] * grads[i] + behind[i] + l_ref[i, m]
    state_of = [state_ref[i, c] for c, i in cases]
    after_of = [after_ref[i, c] for c, i in cases]
    grad_of = [grad_ref[i, c] for c, i in cases]

    fresh = [
        f_ref[i, c] - dot(twice(w_ref[i, c], 1), wide(state, 1), NT)
        for (c, i), state in zip(cases, state_of)
    ]
    fresh_grad = [
        u_ref[i, c]
        + (terms[c]["rk_col"] * h["to_end"]) * dot(twice(ks[c], 1), wide(grad, 1), NT)
        for (c, i), h, grad in zip(cases, gates, grad_of)
    ]
    solved = [
        dot3(t_ref[i, c], x, TN) for (c, i), x in zip(cases, fresh_grad)
    ]
    value_grad = [h["beta_col"] * x for h, x in zip(gates, solved)]
    quarter = (out_refs[0].shape[1] - 128) // 4
    for (c, i), x in zip(cases, value_grad):
        start = 2 * quarter + here * (2 * DV) + i * DV
        out_refs[c][:, pl.ds(pl.multiple_of(start, DV), DV)] = low(x)
    sides = [jnp.concatenate([low(x), o], axis=0) for x, o in zip(value_grad, o_in)]
    fresh_low = [low(x) for x in fresh]
    outer = [dot(x, low(state)) for x, state in zip(sides, state_of)]
    ended = [
        h["to_end"] * dot(x, low(grad)) for h, x, grad in zip(gates, fresh_low, grad_of)
    ]
    inner = [dot(x, y, NT) for x, y in zip(sides, fresh_low)]
    key_read = [-h["growth_col"] * x[:CHUNK] for h, x in zip(gates, outer)]
    query_read = [h["growth_col"] * x[CHUNK:] for h, x in zip(gates, outer)]
    erase = [jnp.where(before, h["decay"] * x[:CHUNK], 0.0) for h, x in zip(gates, inner)]
    read = [h["decay"] * x[CHUNK:] for h, x in zip(gates, inner)]
    units = [(t["qf"] * t["rq_col"], t["kf"] * t["rk_col"]) for t in terms]
    sums = []
    for n, (c, i) in enumerate(cases):
        query_unit, key_unit = units[c]
        spread = read[n] * terms[c]["query_key"] - erase[n] * terms[c]["key_key"]
        lone = query_unit * query_read[n] + key_unit * (key_read[n] - ended[n])
        sums.append(dot(twice(suffix, 1), wide(jnp.concatenate([spread, lone], axis=1), 0)))
    query_inner, key_inner = [], []
    for c in range(chunks):
        term = terms[c]
        read_sum = read[2 * c] + read[2 * c + 1]
        erase_sum = erase[2 * c] + erase[2 * c + 1]
        query_inner.append(dot(wide(read_sum * term["rk_row"], 1), twice(ks[c], 0)))
        key_inner.append(
            dot(wide(erase_sum * -term["rk_row"], 1), twice(ks[c], 0))
            + dot(
                jnp.concatenate(
                    split(read_sum * term["rq_col"]) + split(erase_sum * -term["rk_col"]), axis=0
                ),
                jnp.concatenate([qs[c], qs[c], ks[c], ks[c]], axis=0),
                TN,
            )
        )
    small_out = []
    for c in range(chunks):
        parts, places = [], []
        wholes = 0.0
        for i in range(2):
            n = 2 * c + i
            at = 2 * pair + i
            for place, part in (
                (at, jnp.where(before, sums[n][:, :CHUNK], 0.0) + sums[n][:, CHUNK:]),
                (at + 8, (1.0 - gates[n]["beta_col"]) * solved[n] * fresh[n]),
            ):
                parts += split(part)
                places += [low(jnp.where(col == place, 1.0, 0.0))] * 2
            product = jnp.sum(grad_of[n] * after_of[n], axis=0, keepdims=True)
            whole = jnp.sum(product, axis=1, keepdims=True)
            wholes = wholes + jnp.where(col[:1] == at, whole, 0.0)
        small_out.append(
            dot(jnp.concatenate(parts, axis=1), jnp.concatenate(places, axis=0)) + wholes
        )
    for c in range(chunks):
        term = terms[c]
        query_unit, key_unit = units[c]
        query_grad = query_inner[c] + query_read[2 * c] + query_read[2 * c + 1]
        key_grad = (
            key_inner[c]
            + (key_read[2 * c] + ended[2 * c])
            + (key_read[2 * c + 1] + ended[2 * c + 1])
        )
        query_back = term["rq_col"] * (
            query_grad
            - query_unit * (DK * jnp.sum(query_unit * query_grad, axis=1, keepdims=True))
        )
        key_back = term["rk_col"] * (
            key_grad - key_unit * jnp.sum(key_unit * key_grad, axis=1, keepdims=True)
        )
        out_refs[c][:, pl.ds(pl.multiple_of(here * DK, DK), DK)] = low(query_back)
        out_refs[c][:, pl.ds(pl.multiple_of(quarter + here * DK, DK), DK)] = low(key_back)
        place = slice(4 * quarter, 4 * quarter + 128)
        mine = (col // 2 == pair) | (col // 2 == pair + 4)
        held = out_refs[c][:, place]
        kept = jnp.where(here == 0, jnp.zeros_like(held), held)
        out_refs[c][:, place] = jnp.where(mine, low(small_out[c]), kept)

def pack_kernel(me_ref, *refs):
    outs = refs[-CHUNKS:]
    for slot, out_ref in enumerate(outs):
        at = 0
        for ref in refs[4 * slot : 4 * slot + 4]:
            width = ref.shape[1]
            out_ref[:, at : at + width] = ref[...]
            at += width
    if len(refs) > 5 * CHUNKS:
        d_ref, b_ref = refs[4 * CHUNKS : 4 * CHUNKS + 2]
        for slot, out_ref in enumerate(outs):
            dest = lax.rem(me_ref[0] + slot, CHUNKS)
            row, col = grids((d_ref.shape[0], 128))
            decays = (col < HEADS) & (row == HEADS * dest + col)
            betas = (col >= HEADS) & (col < 2 * HEADS) & (row == HEADS * dest + col - HEADS)
            picks = [low(jnp.where(here, 1.0, 0.0)) for here in (decays, betas)]
            out_ref[:, at : at + 128] = low(
                dot(d_ref[...], picks[0], TN) + dot(b_ref[...], picks[1], TN)
            )

def pack(me, arrays, gates, begin, end):
    count = end - begin
    per = KEY_HEADS // count
    first = begin // count
    widths = [count * size for size in (DK, DK, 2 * DV, 2 * DV)]
    total = sum(widths) + (128 if gates else 0)
    specs = []
    for slot in range(CHUNKS):
        for width in widths:
            specs.append(
                pl.BlockSpec(
                    (CHUNK, width),
                    lambda g, me, slot=slot: (0, per * lax.rem(me[0] + slot, CHUNKS) + first),
                )
            )
    return pl.pallas_call(
        pack_kernel,
        grid_spec=pltpu.PrefetchScalarGridSpec(
            num_scalar_prefetch=1,
            grid=(1,),
            in_specs=specs + [pl.BlockSpec(gate.shape, lambda g, me: (0, 0)) for gate in gates],
            out_specs=[pl.BlockSpec((CHUNK, total), lambda g, me: (0, 0))] * CHUNKS,
        ),
        out_shape=[jax.ShapeDtypeStruct((CHUNK, total), bf16)] * CHUNKS,
        compiler_params=pltpu.CompilerParams(vmem_limit_bytes=VMEM),
        name="pack",
    )(me, *(list(arrays) * CHUNKS), *gates)

def unpack_kernel(me_ref, *refs):
    arrived = refs[: len(GROUPS) * CHUNKS]
    q_ref, k_ref, v_ref, d_ref, b_ref = refs[len(GROUPS) * CHUNKS :]
    d_sum, b_sum = 0.0, 0.0
    row, col = grids((d_ref.shape[0], 128))
    for g, (begin, end) in enumerate(GROUPS):
        for slot in range(CHUNKS):
            ref = arrived[g * CHUNKS + slot]
            source = lax.rem(me_ref[0] + slot, CHUNKS)
            at = 0
            for out, size in ((q_ref, DK), (k_ref, DK), (v_ref, 2 * DV)):
                width = (end - begin) * size
                start = pl.multiple_of((source * KEY_HEADS + begin) * size, 128)
                out[:, pl.ds(start, width)] = ref[:, at : at + width]
                at += width
            small = ref[:, at : at + 128]
            decays = (col < HEADS) & (row == HEADS * source + col)
            betas = (col >= HEADS) & (col < 2 * HEADS) & (row == HEADS * source + col - HEADS)
            d_sum = d_sum + dot(low(jnp.where(decays, 1.0, 0.0)), small, NT)
            b_sum = b_sum + dot(low(jnp.where(betas, 1.0, 0.0)), small, NT)
    d_ref[...] = low(d_sum)
    b_ref[...] = low(b_sum)

def whole(shape):
    return pl.BlockSpec(shape, lambda g, me: (0,) * len(shape))

def unpack(me, groups):
    arrived = [x for group in groups for x in group]
    shapes = [(CHUNK, CHUNKS * size) for size in (KEY_HEADS * DK, KEY_HEADS * DK, HEADS * DV)]
    shapes += [(CHUNKS * HEADS, CHUNK)] * 2
    q, k, v, d, b = pl.pallas_call(
        unpack_kernel,
        grid_spec=pltpu.PrefetchScalarGridSpec(
            num_scalar_prefetch=1,
            grid=(1,),
            in_specs=[whole(x.shape) for x in arrived],
            out_specs=[whole(shape) for shape in shapes],
        ),
        out_shape=[jax.ShapeDtypeStruct(shape, bf16) for shape in shapes],
        compiler_params=pltpu.CompilerParams(vmem_limit_bytes=VMEM),
        name="unpack",
    )(me, *arrived)
    return q, k, v, d.T, b.T

def packed_specs(count, small_at, off=0):
    return (
        [pl.BlockSpec((CHUNK, DK), lambda p, me: (0, off + p))] * CHUNKS
        + [pl.BlockSpec((CHUNK, DK), lambda p, me: (0, count + off + p))] * CHUNKS
        + [pl.BlockSpec((CHUNK, 2 * DV), lambda p, me: (0, count + off + p))] * CHUNKS
        + [pl.BlockSpec((CHUNK, 2 * DV), lambda p, me: (0, 2 * count + off + p))] * CHUNKS
        + [pl.BlockSpec((CHUNK, 128), lambda p, me: (0, small_at))] * CHUNKS
    )

SAVED = (bf16, f32, f32, f32, bf16, f32, f32)

def saved_specs(off=0):
    square = (2, CHUNKS, CHUNK, CHUNK)
    return [pl.BlockSpec(square, lambda p, me: (off + p, 0, 0, 0)) for _ in SAVED]

def cost(count, flops):
    return pl.CostEstimate(flops=count * flops, bytes_accessed=count * 5_000_000, transcendentals=0)

def local_pass(me, packed, small, small_at, begin, end):
    count = end - begin
    return pl.pallas_call(
        functools.partial(local_kernel, begin),
        grid_spec=pltpu.PrefetchScalarGridSpec(
            num_scalar_prefetch=1,
            grid=(count,),
            in_specs=packed_specs(count, small_at),
            out_specs=[pl.BlockSpec((2, 2, PAYLOAD, DK), lambda p, me: (p, 0, 0, 0))] + saved_specs(),
        ),
        out_shape=[jax.ShapeDtypeStruct((2 * count, 2, PAYLOAD, DK), bf16)]
        + [jax.ShapeDtypeStruct((2 * count, CHUNKS, CHUNK, CHUNK), kind) for kind in SAVED],
        compiler_params=pltpu.CompilerParams(vmem_limit_bytes=VMEM),
        cost_estimate=cost(count, 4_000_000_000),
        name="local_pass",
    )(me, *(list(packed) * 4), *small)

def combine_pass(place, received):
    shape = (DK + DV + 8, DK)
    each = (received.shape[0],) + shape
    return pl.pallas_call(
        combine_kernel,
        grid_spec=pltpu.PrefetchScalarGridSpec(
            num_scalar_prefetch=1,
            grid=(1,),
            in_specs=[whole(received.shape)],
            out_specs=[whole(shape), whole(each)],
        ),
        out_shape=[jax.ShapeDtypeStruct(shape, f32), jax.ShapeDtypeStruct(each, f32)],
        compiler_params=pltpu.CompilerParams(vmem_limit_bytes=VMEM),
        cost_estimate=cost(1, 1_500_000_000),
        name="combine_pass",
    )(place, received)

def chain_pass(place, before, others):
    shape = (before.shape[0], DV, DK)
    return pl.pallas_call(
        chain_kernel,
        grid_spec=pltpu.PrefetchScalarGridSpec(
            num_scalar_prefetch=1,
            grid=(1,),
            in_specs=[whole(before.shape)] + [whole(x.shape) for x in others],
            out_specs=whole(shape),
        ),
        out_shape=jax.ShapeDtypeStruct(shape, bf16),
        compiler_params=pltpu.CompilerParams(vmem_limit_bytes=VMEM),
        cost_estimate=cost(1, 1_500_000_000),
        name="chain_pass",
    )(place, before, *others)

def final_pass(me, packed, small, small_at, saved, states, group, begin, end):
    count = end - begin
    held, off = group[1] - group[0], begin - group[0]
    width = count * 2 * (DK + DV) + 128
    square = (2, CHUNKS, DV, DK)
    return pl.pallas_call(
        functools.partial(final_kernel, begin),
        grid_spec=pltpu.PrefetchScalarGridSpec(
            num_scalar_prefetch=1,
            grid=(count,),
            in_specs=packed_specs(held, small_at, off)
            + saved_specs(off)
            + [pl.BlockSpec((2, 2, DV, DK), lambda p, me: (off + p, 0, 0, 0))],
            out_specs=[pl.BlockSpec((CHUNK, width), lambda p, me: (0, 0))] * CHUNKS,
            scratch_shapes=[pltpu.VMEM((2, CHUNKS, 8, DK), f32)] + [pltpu.VMEM(square, f32)] * 3,
        ),
        out_shape=[jax.ShapeDtypeStruct((CHUNK, width), bf16)] * CHUNKS,
        compiler_params=pltpu.CompilerParams(vmem_limit_bytes=VMEM),
        cost_estimate=cost(count, 4_000_000_000),
        name="final_pass",
    )(me, *(list(packed) * 4), *small, *saved, states)

def turned(slots, way):
    count = lax.axis_size("head")
    return [slots[0]] + [
        lax.ppermute(slots[s], "head", [(i, (i + way * s) % count) for i in range(count)])
        for s in range(1, count)
    ]

def recursion(sends, place):
    segments = lax.axis_size("ctx")
    rows = segments // HEADS
    near = [[y * HEADS + r for r in range(HEADS)] for y in range(rows)]
    received = lax.all_to_all(
        sends, "ctx", split_axis=0, concat_axis=0, axis_index_groups=near, tiled=True
    )
    combined, before = combine_pass(place, received)
    others = [
        lax.ppermute(
            combined, "ctx", [(i, (i + s * HEADS) % segments) for i in range(segments)]
        )
        for s in range(1, rows)
    ]
    return lax.all_to_all(
        chain_pass(place, before, others),
        "ctx",
        split_axis=0,
        concat_axis=0,
        axis_index_groups=near,
        tiled=True,
    )

def on_device(query_rows, key_rows, value_rows, log_decay, beta_logit, out_grad):
    arrays = [query_rows, key_rows, value_rows, out_grad]
    gates = [log_decay.T, beta_logit.T]
    me = lax.axis_index("head").astype(jnp.int32).reshape(1)
    segment = lax.axis_index("ctx").astype(jnp.int32)
    rows = lax.axis_size("ctx") // HEADS
    place = jnp.stack([segment % 2, segment // HEADS, jnp.int32(rows)])
    received = []
    for b, e in GROUPS:
        slots = pack(me, arrays, gates if b == 0 else [], b, e)
        if received:
            slots, received[-1], place = lax.optimization_barrier((slots, received[-1], place))
        received.append(turned(slots, 1))
    small = received[0]
    small_at = small[0].shape[1] // 128 - 1
    saved, states, outs = [], [], []
    for (b, e), packed in zip(GROUPS, received):
        sends, *kept = local_pass(me, packed, small, small_at, b, e)
        saved.append(kept)
        found = recursion(sends.reshape(HEADS, PAYLOAD, DK), place)
        states.append(found.reshape(2 * (e - b), 2, DV, DK))
    for b, e in GROUPS:
        n = [g for g, (first, last) in enumerate(GROUPS) if first <= b < last][0]
        grads = final_pass(
            me, received[n], small, small_at, saved[n], states[n], GROUPS[n], b, e
        )
        outs.append(turned(grads, -1))
    return unpack(me, outs)

def solution(mesh):
    spec = P(("ctx", "head"), None)
    return jax.shard_map(
        on_device, mesh=mesh, in_specs=(spec,) * 6, out_specs=(spec,) * 5, check_vma=False
    )
```
